128 devices in a mesh: fsdp: 16 (over y, x), row: 8 (over z, core).
Axes of the slice: x: 4, y: 4, z: 4, core: 2. Of those that a mesh axis runs over, the one named last changes fastest.
Arguments:
- grad_gate: bfloat16 [25600, 5120], P('row', 'fsdp'), may hold values from -400 to 400
- grad_up: bfloat16 [25600, 5120], P('row', 'fsdp'), may hold values from -400 to 400
- grad_down: bfloat16 [5120, 25600], P('row', 'fsdp'), may hold values from -400 to 400
- proj_gate: bfloat16 [256, 5120], P(None, 'fsdp'), may hold values from -0.375 to 0.375
- proj_up: bfloat16 [256, 5120], P(None, 'fsdp'), may hold values from -0.375 to 0.375
- proj_down: bfloat16 [256, 5120], P(None, 'row'), may hold values from -0.375 to 0.375
- first_gate: float32 [256, 25600], P('fsdp', 'row'), may hold values from -800 to 800
- second_gate: float32 [256, 25600], P('fsdp', 'row'), may hold values from 400 to 40000
- first_up: float32 [256, 25600], P('fsdp', 'row'), may hold values from -800 to 800
- second_up: float32 [256, 25600], P('fsdp', 'row'), may hold values from 400 to 40000
- first_down: float32 [256, 25600], P('row', 'fsdp'), may hold values from -800 to 800
- second_down: float32 [256, 25600], P('row', 'fsdp'), may hold values from 400 to 40000
Outputs:
- update_gate: bfloat16 [25600, 5120], P('row', 'fsdp')
- update_up: bfloat16 [25600, 5120], P('row', 'fsdp')
- update_down: bfloat16 [5120, 25600], P('row', 'fsdp')
- first_gate_new: float32 [256, 25600], P('fsdp', 'row')
- second_gate_new: float32 [256, 25600], P('fsdp', 'row')
- first_up_new: float32 [256, 25600], P('fsdp', 'row')
- second_up_new: float32 [256, 25600], P('fsdp', 'row')
- first_down_new: float32 [256, 25600], P('row', 'fsdp')
- second_down_new: float32 [256, 25600], P('row', 'fsdp')
The draws below stay inside these ranges and needn't reach their ends.
All inputs are finite; a program needn't handle non-finite values.
Results may differ from the reference program's by a relative error of at most 0.015.
Values may be sent and summed in bfloat16 or wider, within the bound.
No kernel may reach another device: no remote copies, remote signals or barrier semaphores. Data moves between devices by JAX's collectives and lax.ppermute only.
A program may use at most 64 MiB of HBM per device.

```python
import math
import jax
import jax.numpy as jnp
from jax import lax

D = 5120
FF = 25600
RANK = 256
STEP = 100
N_FSDP = 16
N_ROW = 8


def scaled(key, rows_count, cols_count):
    row_key, col_key = jax.random.split(key)
    row_scale = jnp.exp(jax.random.uniform(row_key, (rows_count, 1), jnp.float32) * math.log(10.0))
    col_scale = jnp.exp(jax.random.uniform(col_key, (1, cols_count), jnp.float32) * math.log(10.0))
    return row_scale * col_scale


def ramped(key, rows_count, cols_count, rise_factor):
    rank_ramp = 1.0 + rise_factor * jnp.arange(rows_count, dtype=jnp.float32)[:, None] / (rows_count - 1)
    base_noise = jax.random.truncated_normal(key, -4.0, 4.0, (rows_count, cols_count), jnp.float32)
    return 40.0 * base_noise * rank_ramp


def draw_grad_gate(key, part):
    key = jax.random.fold_in(key, 11)
    noise_key, scale_key = jax.random.split(key)
    base_noise = jax.random.truncated_normal(noise_key, -4.0, 4.0, (FF, D), jnp.float32)
    return (base_noise * scaled(scale_key, FF, D)).astype(jnp.bfloat16)


def draw_grad_up(key, part):
    key = jax.random.fold_in(key, 12)
    noise_key, scale_key = jax.random.split(key)
    base_noise = jax.random.truncated_normal(noise_key, -4.0, 4.0, (FF, D), jnp.float32)
    return (base_noise * scaled(scale_key, FF, D)).astype(jnp.bfloat16)


def draw_grad_down(key, part):
    key = jax.random.fold_in(key, 13)
    noise_key, scale_key = jax.random.split(key)
    base_noise = jax.random.truncated_normal(noise_key, -4.0, 4.0, (D, FF), jnp.float32)
    return (base_noise * scaled(scale_key, D, FF)).astype(jnp.bfloat16)


def draw_first_gate(key, part):
    key = jax.random.fold_in(key, 21)
    return ramped(key, RANK, FF, 2.0)


def draw_first_up(key, part):
    key = jax.random.fold_in(key, 22)
    return ramped(key, RANK, FF, 2.0)


def draw_first_down(key, part):
    key = jax.random.fold_in(key, 23)
    return ramped(key, RANK, FF, 2.0)


def levels(key, dims, cuts, low, high):
    def one(axis_at, parts):
        draws = jax.random.uniform(jax.random.fold_in(jax.random.fold_in(key, 6), axis_at), (parts,), jnp.float32, low / len(cuts), high / len(cuts))
        return jnp.repeat(jnp.exp(draws), dims[axis_at] // parts).reshape((-1,) + (1,) * (len(dims) - axis_at - 1))

    gain = one(*cuts[0])
    for cut in cuts[1:]:
        gain = gain * one(*cut)
    return gain


def scatter_about(own_key, extent, scale, limit, cuts=(), held_as=jnp.bfloat16):
    gain = levels(own_key, extent, cuts, -0.22, 0.18) if cuts else 1.0
    values = jax.random.normal(own_key, extent, jnp.float32) * scale * gain
    return jnp.minimum(jnp.maximum(values, -limit), limit).astype(held_as)


def setup_inputs(seed: int = 0) -> dict:
    splits = jax.random.split(jax.random.key(seed), 13)
    grad_gate = draw_grad_gate(jax.random.fold_in(splits[12], 71), 0)
    grad_up = draw_grad_up(jax.random.fold_in(splits[12], 71), 0)
    grad_down = draw_grad_down(jax.random.fold_in(splits[12], 71), 0)
    proj_gate = scatter_about(splits[3], (RANK, D), RANK ** -0.5, 0.375, ((1, 16),))
    proj_up = scatter_about(splits[4], (RANK, D), RANK ** -0.5, 0.375, ((1, 16),))
    proj_down = scatter_about(splits[5], (RANK, D), RANK ** -0.5, 0.375, ((1, 8),))
    first_gate = draw_first_gate(jax.random.fold_in(splits[12], 71), 0)
    second_gate = jnp.clip(jnp.exp(math.log(40000.0) - 4.6051702 * jax.random.uniform(splits[7], (RANK, FF), jnp.float32) ** levels(splits[7], (RANK, FF), ((0, 16), (1, 8)), -0.2, 0.2)), 400.0, 40000.0)
    first_up = draw_first_up(jax.random.fold_in(splits[12], 71), 0)
    second_up = jnp.clip(jnp.exp(math.log(40000.0) - 4.6051702 * jax.random.uniform(splits[9], (RANK, FF), jnp.float32) ** levels(splits[9], (RANK, FF), ((0, 16), (1, 8)), -0.2, 0.2)), 400.0, 40000.0)
    first_down = draw_first_down(jax.random.fold_in(splits[12], 71), 0)
    second_down = jnp.clip(jnp.exp(math.log(40000.0) - 4.6051702 * jax.random.uniform(splits[11], (RANK, FF), jnp.float32) ** levels(splits[11], (RANK, FF), ((0, 8), (1, 16)), -0.2, 0.2)), 400.0, 40000.0)
    return {"grad_gate": grad_gate, "grad_up": grad_up, "grad_down": grad_down, "proj_gate": proj_gate, "proj_up": proj_up, "proj_down": proj_down, "first_gate": first_gate, "second_gate": second_gate, "first_up": first_up, "second_up": second_up, "first_down": first_down, "second_down": second_down}


beta_first = 0.9
beta_second = 0.999
adam_epsilon = 1e-08
norm_epsilon = 1e-06
update_scale = 4.0

def narrowed(block_value):
    held_value = block_value.astype(jnp.bfloat16)
    held_value = lax.optimization_barrier(held_value)
    return held_value.astype(jnp.float32)

def project_columns(gradient, projection, groups):
    block_width = gradient.shape[1] // groups

    def add_block(block_index, running):
        block_start = (block_index * block_width).astype(jnp.int32)
        proj_block = lax.dynamic_slice_in_dim(projection, block_start, block_width, 1)
        grad_block = lax.dynamic_slice_in_dim(gradient, block_start, block_width, 1)
        block_term = lax.dot_general(proj_block, grad_block, (((1,), (1,)), ((), ())), preferred_element_type=jnp.float32)
        return running + narrowed(block_term)
    start_sum = jnp.zeros((projection.shape[0], gradient.shape[0]), jnp.float32)
    return lax.fori_loop(0, groups, add_block, start_sum)

def project_rows(gradient, projection, groups):
    block_width = gradient.shape[0] // groups

    def add_block(block_index, running):
        block_start = (block_index * block_width).astype(jnp.int32)
        proj_block = lax.dynamic_slice_in_dim(projection, block_start, block_width, 1)
        grad_block = lax.dynamic_slice_in_dim(gradient, block_start, block_width, 0)
        block_term = jnp.dot(proj_block, grad_block, preferred_element_type=jnp.float32)
        return running + narrowed(block_term)
    start_sum = jnp.zeros((projection.shape[0], gradient.shape[1]), jnp.float32)
    return lax.fori_loop(0, groups, add_block, start_sum)

def moments(projected, first_moment, second_moment):
    first_new = beta_first * first_moment + (1.0 - beta_first) * projected
    second_new = beta_second * second_moment + (1.0 - beta_second) * projected * projected
    corrected = first_new / (1.0 - beta_first ** STEP) / (jnp.sqrt(second_new / (1.0 - beta_second ** STEP)) + adam_epsilon)
    channel_scale = jnp.sqrt(lax.optimization_barrier(jnp.sum(corrected * corrected, 0))) / (jnp.sqrt(lax.optimization_barrier(jnp.sum(projected * projected, 0))) + norm_epsilon)
    return (first_new, second_new, channel_scale)

def reference(grad_gate, grad_up, grad_down, proj_gate, proj_up, proj_down, first_gate, second_gate, first_up, second_up, first_down, second_down):
    gate_projected = project_columns(grad_gate, proj_gate, N_FSDP)
    up_projected = project_columns(grad_up, proj_up, N_FSDP)
    down_projected = project_rows(grad_down, proj_down, N_ROW)
    first_gate_new, second_gate_new, gate_scale = moments(gate_projected, first_gate, second_gate)
    first_up_new, second_up_new, up_scale = moments(up_projected, first_up, second_up)
    first_down_new, second_down_new, down_scale = moments(down_projected, first_down, second_down)
    update_gate = (update_scale * grad_gate.astype(jnp.float32) * gate_scale[:, None]).astype(jnp.bfloat16)
    update_up = (update_scale * grad_up.astype(jnp.float32) * up_scale[:, None]).astype(jnp.bfloat16)
    update_down = (update_scale * grad_down.astype(jnp.float32) * down_scale[None, :]).astype(jnp.bfloat16)
    return (update_gate, update_up, update_down, first_gate_new, second_gate_new, first_up_new, second_up_new, first_down_new, second_down_new)
```

```python
import jax
import jax.numpy as jnp
from jax import lax
from jax.sharding import Mesh
from jax.sharding import PartitionSpec as P

STEP = 100

beta_first = 0.9
beta_second = 0.999
adam_epsilon = 1e-08
norm_epsilon = 1e-06
update_scale = 4.0

AXES = ("y", "x", "z", "core")
SIZES = (4, 4, 4, 2)
ALONG = ("y", "x")
ACROSS = ("z", "core")


def adam_step(own_rows, first_moment, second_moment):
    first_new = beta_first * first_moment + (1.0 - beta_first) * own_rows
    second_new = beta_second * second_moment + (1.0 - beta_second) * own_rows * own_rows
    corrected = (
        first_new
        / (1.0 - beta_first**STEP)
        / (jnp.sqrt(second_new / (1.0 - beta_second**STEP)) + adam_epsilon)
    )
    return (first_new, second_new, corrected)


def against_features(projection, gradient):
    return lax.dot_general(
        projection, gradient, (((1,), (1,)), ((), ())), preferred_element_type=jnp.float32
    )


def device_number(y, x, z, core):
    return ((y * 4 + x) * 4 + z) * 2 + core


def ring_pairs(shift, stage):
    pairs = []
    for y in range(4):
        for x in range(4):
            for z in range(4):
                for core in range(2):
                    source = device_number(y, x, z, core)
                    if (core == 0) == (stage == 0):
                        target = device_number(y, (x + shift) % 4, z, core)
                    else:
                        target = device_number((y + shift) % 4, x, z, core)
                    pairs.append((source, target))
    return pairs


def ring_send(value, shift, stage):
    return lax.ppermute(value, AXES, ring_pairs(shift, stage))


def z_send(value, shift):
    return lax.ppermute(value, "z", [(i, (i + shift) % 4) for i in range(4)])


def core_send(value):
    return lax.ppermute(value, "core", [(0, 1), (1, 0)])


def add(*terms):
    total = terms[0].astype(jnp.float32)
    for term in terms[1:]:
        total = total + term.astype(jnp.float32)
    return total


def pick_rows(projection, rows):
    chosen = (rows[:, None] == jnp.arange(projection.shape[0])[None, :]).astype(projection.dtype)
    return jnp.dot(chosen, projection, preferred_element_type=jnp.float32).astype(projection.dtype)


def ring_reduce(forth, back, near, far, keep):
    half = keep.shape[0] // 2
    from_below = ring_send(forth, 1, 0)
    from_above = ring_send(back, 3, 0)
    onward = add(near, from_below[half:]).astype(jnp.bfloat16)
    backward = add(far, from_above[:half]).astype(jnp.bfloat16)
    last_below = ring_send(onward, 1, 0)
    last_above = ring_send(backward, 3, 0)
    last_below, last_above = lax.optimization_barrier((last_below, last_above))
    low = add(keep[:half], from_above[half:], last_below)
    high = add(keep[half:], from_below[:half], last_above)
    return low, high


def per_device(
    grad_gate,
    grad_up,
    grad_down,
    proj_gate,
    proj_up,
    proj_down,
    first_gate,
    second_gate,
    first_up,
    second_up,
    first_down,
    second_down,
):
    y, x, z, core = (lax.axis_index(name) for name in AXES)
    local_ff = grad_gate.shape[0]
    step = jnp.arange(256)
    outer, inner = step // 64, step // 16 % 4
    on_x, on_y = jnp.where(core == 0, outer, inner), jnp.where(core == 0, inner, outer)
    rows = ((y + on_y) % 4 * 4 + (x + on_x) % 4) * 16 + step % 16
    down_rows = ((z + step // 32 % 4) % 4 * 2 + (core + step // 128) % 2) * 32 + step % 32

    reduced = []
    for gradient, projection in ((grad_gate, proj_gate), (grad_up, proj_up)):
        ordered = pick_rows(projection, rows)
        sent = against_features(ordered[96:224], gradient).astype(jnp.bfloat16)
        rest = against_features(
            jnp.concatenate((ordered[:96], ordered[224:])), gradient
        ).astype(jnp.bfloat16)
        reduced.append(ring_reduce(sent[:64], sent[64:], rest[64:96], rest[96:], rest[:64]))
    low = jnp.concatenate((reduced[0][0], reduced[1][0]), 1)
    high = jnp.concatenate((reduced[0][1], reduced[1][1]), 1)
    opposite = ring_send(high[:16].astype(jnp.bfloat16), 2, 1)
    above = ring_send(high[16:].astype(jnp.bfloat16), 3, 1)
    below = ring_send(low[16:].astype(jnp.bfloat16), 1, 1)
    own_rows = add(low[:16], opposite, above, below)
    first_pair = jnp.concatenate((first_gate, first_up), 1)
    second_pair = jnp.concatenate((second_gate, second_up), 1)
    pair_first, pair_second, corrected = adam_step(own_rows, first_pair, second_pair)
    sums = jnp.stack((jnp.sum(corrected * corrected, 0), jnp.sum(own_rows * own_rows, 0)))
    for stage in (1, 0):
        sums = sums + (ring_send(sums, 2, stage) + ring_send(sums, 1, stage) + ring_send(sums, 3, stage))
    pair_scale = update_scale * jnp.sqrt(sums[0]) / (jnp.sqrt(sums[1]) + norm_epsilon)
    update_gate = (grad_gate.astype(jnp.float32) * pair_scale[:local_ff, None]).astype(jnp.bfloat16)
    update_up = (grad_up.astype(jnp.float32) * pair_scale[local_ff:, None]).astype(jnp.bfloat16)

    partial_down = jnp.dot(
        pick_rows(proj_down, down_rows), grad_down, preferred_element_type=jnp.float32
    ).astype(jnp.bfloat16)
    down_sum = add(partial_down[:128], core_send(partial_down[128:])).astype(jnp.bfloat16)
    own_down = add(
        down_sum[:32],
        z_send(down_sum[64:96], 2),
        z_send(down_sum[32:64], 1),
        z_send(down_sum[96:], 3),
    )
    first_down_new, second_down_new, corrected_down = adam_step(own_down, first_down, second_down)
    down_sums = jnp.stack((jnp.sum(corrected_down * corrected_down, 0), jnp.sum(own_down * own_down, 0)))
    down_sums = down_sums + core_send(down_sums)
    down_sums = down_sums + (z_send(down_sums, 2) + z_send(down_sums, 1) + z_send(down_sums, 3))
    down_scale = update_scale * jnp.sqrt(down_sums[0]) / (jnp.sqrt(down_sums[1]) + norm_epsilon)
    update_down = (grad_down.astype(jnp.float32) * down_scale[None, :]).astype(jnp.bfloat16)
    return (
        update_gate,
        update_up,
        update_down,
        pair_first[:, :local_ff],
        pair_second[:, :local_ff],
        pair_first[:, local_ff:],
        pair_second[:, local_ff:],
        first_down_new,
        second_down_new,
    )


def solution(mesh):
    fine = Mesh(mesh.devices.reshape(SIZES), AXES)
    gradient, state = P(ACROSS, ALONG), P(ALONG, ACROSS)
    return jax.shard_map(
        per_device,
        mesh=fine,
        in_specs=(
            gradient,
            gradient,
            gradient,
            P(None, ALONG),
            P(None, ALONG),
            P(None, ACROSS),
            state,
            state,
            state,
            state,
            gradient,
            gradient,
        ),
        out_specs=(
            gradient,
            gradient,
            gradient,
            state,
            state,
            state,
            state,
            gradient,
            gradient,
        ),
        check_vma=False,
    )
```

```python
import jax
import jax.numpy as jnp
from jax import lax
from jax.experimental import pallas as pl
from jax.experimental.pallas import tpu as pltpu
from jax.sharding import Mesh
from jax.sharding import PartitionSpec as P

STEP = 100

beta_first = 0.9
beta_second = 0.999
adam_epsilon = 1e-08
norm_epsilon = 1e-06
update_scale = 4.0

AXES = ("y", "x", "z", "core")
SIZES = (4, 4, 4, 2)
ALONG = ("y", "x")
ACROSS = ("z", "core")
F32 = jnp.float32
BF16 = jnp.bfloat16


def device_number(y, x, z, core):
    return ((y * 4 + x) * 4 + z) * 2 + core


def ring_pairs(shift, stage):
    pairs = []
    for y in range(4):
        for x in range(4):
            for z in range(4):
                for core in range(2):
                    source = device_number(y, x, z, core)
                    if (core == 0) == (stage == 0):
                        target = device_number(y, (x + shift) % 4, z, core)
                    else:
                        target = device_number((y + shift) % 4, x, z, core)
                    pairs.append((source, target))
    return pairs


def ring_send(value, shift, stage):
    return lax.ppermute(value, AXES, ring_pairs(shift, stage))


def z_swap(value, far):
    pairs = [(0, 3), (3, 0), (1, 2), (2, 1)] if far else [(0, 1), (1, 0), (2, 3), (3, 2)]
    return lax.ppermute(value, "z", pairs)


def core_send(value):
    return lax.ppermute(value, "core", [(0, 1), (1, 0)])


VMEM = pl.BlockSpec(memory_space=pltpu.VMEM)
HBM = pl.BlockSpec(memory_space=pltpu.HBM)


class Chain:
    def __init__(self):
        self.last = None

    def __call__(self, body, outs, *operands, in_specs=None, out_specs=None, scratch=(), limit=8):
        specs = [VMEM] * len(operands) if in_specs is None else list(in_specs)
        count, made = len(operands), len(outs)
        if self.last is not None:
            operands = operands + (self.last,)
            specs.append(VMEM)
        operands = [
            pltpu.with_memory_space_constraint(operand, spec.memory_space)
            for operand, spec in zip(operands, specs)
        ]

        def kernel(*refs):
            refs, token = refs[: len(operands)], refs[len(operands) :]
            token, rest = token[made], token[:made] + token[made + 1 :]
            token[...] = jnp.zeros_like(token)
            body(*refs[:count], *rest)

        *result, self.last = pl.pallas_call(
            kernel,
            out_shape=[*outs, pltpu.VMEM((8, 128), F32)],
            in_specs=specs,
            out_specs=[*([VMEM] * made if out_specs is None else out_specs), VMEM],
            scratch_shapes=scratch,
            compiler_params=pltpu.CompilerParams(vmem_limit_bytes=limit * 2**20),
            cost_estimate=pl.CostEstimate(flops=0, bytes_accessed=0, transcendentals=0),
        )(*operands)
        return result


def wide(*terms):
    total = terms[0].astype(F32)
    for term in terms[1:]:
        total = total + term.astype(F32)
    return total


def picked(rows, projection, contract):
    place = lax.broadcasted_iota(jnp.int32, (256, 256), 1)
    chosen = jnp.where(rows == place, 1.0, 0.0).astype(BF16)
    return lax.dot_general(chosen, projection, (((1,), (contract,)), ((), ())), preferred_element_type=F32).astype(BF16)


def fsdp_rows():
    y, x, core = lax.axis_index("y"), lax.axis_index("x"), lax.axis_index("core")
    step = lax.broadcasted_iota(jnp.int32, (256, 1), 0)
    outer, inner = step // 64, step // 16 % 4
    outer = jnp.where(outer == 0, 2, jnp.where(outer == 3, 0, jnp.where(outer == 1, 1, 3)))
    on_x, on_y = jnp.where(core == 0, outer, inner), jnp.where(core == 0, inner, outer)
    return ((y + on_y) % 4 * 4 + (x + on_x) % 4) * 16 + step % 16


def row_rows():
    z, core = lax.axis_index("z"), lax.axis_index("core")
    step = lax.broadcasted_iota(jnp.int32, (256, 1), 0)
    turn = step // 32 % 4
    to = jnp.where(turn % 2 == 0, z, 3 - z)
    to = jnp.where(turn < 2, to, to + 1 - to % 2 * 2)
    return (to * 2 + (core + step // 128) % 2) * 32 + step % 32


PARTS = tuple(range(0, 3200, 640))


def first_kernel(gate_proj, gate, up_proj, up, forth, back, gate_rest, up_rest, gate_kept, up_kept, projs, sems):
    copies = []
    for index, source in enumerate((gate_proj, up_proj)):
        copies.append(pltpu.make_async_copy(source, projs.at[index], sems.at[index]))
    for index, (source, target) in enumerate(((gate, gate_kept), (up, up_kept))):
        for number, at in enumerate(PARTS):
            to = pl.ds(at, 640)
            sem = sems.at[2 + index * 5 + number]
            copies.append(pltpu.make_async_copy(source.at[:, to], target.at[:, to], sem))
    for copy in copies:
        copy.start()
    rows = fsdp_rows()
    copies[0].wait()
    copies[1].wait()
    for index, (rest, kept) in enumerate(((gate_rest, gate_kept), (up_rest, up_kept))):
        ordered = picked(rows, projs[index], 1)
        rest[...] = ordered[64:]
        for number, at in enumerate(PARTS):
            copies[2 + index * 5 + number].wait()
            part = jnp.dot(ordered[:64], kept[:, at : at + 640], preferred_element_type=F32).astype(BF16)
            base = index * 3200 + at
            forth[:, base : base + 640] = part[:32]
            back[:, base : base + 640] = part[32:]


def rest_kernel(gate_rest, gate, up_rest, up, forth, back, near, far, keep):
    for rest, grad, base in ((gate_rest, gate, 0), (up_rest, up, 3200)):
        for at in range(0, 3200, 640):
            to = slice(base + at, base + at + 640)
            part = jnp.dot(rest[...], grad[:, at : at + 640], preferred_element_type=F32).astype(BF16)
            near[:, to] = part[:32]
            forth[:, to] = part[32:64]
            back[:, to] = part[64:96]
            far[:, to] = part[96:128]
            keep[:, to] = part[128:]


def pass_kernel(near, from_below, far, from_above, onward, backward):
    onward[...] = wide(near[...], from_below[...]).astype(BF16)
    backward[...] = wide(far[...], from_above[...]).astype(BF16)


def gather_kernel(keep, low_above, low_below, high_below, high_above, opposite, above, below, own):
    low = wide(keep[:32], low_above[...], low_below[...])
    high = wide(keep[32:], high_below[...], high_above[...])
    own[...] = low[:16]
    above[...] = low[16:].astype(BF16)
    opposite[...] = high[:16].astype(BF16)
    below[...] = high[16:].astype(BF16)


def moments(projected, first, second):
    return (
        beta_first * first[...] + (1.0 - beta_first) * projected,
        beta_second * second[...] + (1.0 - beta_second) * projected * projected,
    )


def channel_sums(projected, first, second):
    first_value, second_value = moments(projected, first, second)
    corrected = (
        first_value
        / (1.0 - beta_first**STEP)
        / (jnp.sqrt(second_value / (1.0 - beta_second**STEP)) + adam_epsilon)
    )
    return jnp.sum(corrected * corrected, 0, keepdims=True), jnp.sum(projected * projected, 0, keepdims=True)


def pair_sum_kernel(own, a, b, c, first_gate, second_gate, first_up, second_up, sums, total):
    projected = wide(own[...], a[...], b[...], c[...])
    total[...] = projected
    sums[0:1], sums[1:2] = channel_sums(projected[:, :3200], first_gate, second_gate)
    sums[2:3], sums[3:4] = channel_sums(projected[:, 3200:], first_up, second_up)


def pair_moment_kernel(total, first_gate, second_gate, first_up, second_up, *news):
    news[0][...], news[1][...] = moments(total[:, :3200], first_gate, second_gate)
    news[2][...], news[3][...] = moments(total[:, 3200:], first_up, second_up)


def down_sum_kernel(own, other, first, second, sums, total):
    projected = wide(own[...], other[...])
    total[...] = projected
    sums[0:1], sums[1:2] = channel_sums(projected, first, second)


def down_moment_kernel(total, first, second, *news):
    news[0][...], news[1][...] = moments(total[...], first, second)


def add_kernel(*refs):
    refs[-1][...] = wide(*(ref[...] for ref in refs[:-1]))


def scale_of(corrected_sq, projected_sq):
    return update_scale * (jnp.sqrt(corrected_sq) / (jnp.sqrt(projected_sq) + norm_epsilon))


def update_kernel(gate, up, a, b, c, d, gate_out, up_out, gate_made, up_made, sems):
    sums = wide(a[...], b[...], c[...], d[...])
    copies = []
    for index, (grad, made, out) in enumerate(((gate, gate_made, gate_out), (up, up_made, up_out))):
        scale = scale_of(sums[2 * index : 2 * index + 1], sums[2 * index + 1 : 2 * index + 2])
        for number in range(5):
            rows = pl.ds(number * 64, 64)
            made[rows, :] = (grad[rows, :].astype(F32) * scale).astype(BF16)
            copies.append(pltpu.make_async_copy(made.at[rows], out.at[rows], sems.at[index * 5 + number]))
            copies[-1].start()
    for copy in copies:
        copy.wait()


def down_kernel(proj, grad, own, other):
    ordered = picked(row_rows(), proj[...], 0)
    for at, size in ((0, 512), (512, 512), (1024, 576)):
        part = lax.dot_general(
            ordered, grad[at : at + size], (((1,), (1,)), ((), ())), preferred_element_type=F32
        ).astype(BF16)
        own[:, at : at + size] = part[:128]
        other[:, at : at + size] = part[128:]


def down_split_kernel(own, other, keep, send):
    total = wide(own[...], other[...])
    keep[...] = total[:64]
    send[...] = total[64:].astype(BF16)


def down_halve_kernel(own, other, keep, send):
    total = wide(own[...], other[...])
    keep[...] = total[:32]
    send[...] = total[32:].astype(BF16)


def down_update_kernel(grad, own, other, out, scale):
    sums = wide(own[...], other[...])
    scale[:, :1600] = scale_of(sums[0:1], sums[1:2])
    for at in range(0, 1600, 128):
        size = min(128, 1600 - at)
        column = jnp.broadcast_to(scale[:, at : at + 128], (128, 128)).T[:size]
        for lane in range(0, 640, 128):
            block = grad[at : at + size, lane : lane + 128].astype(F32) * column
            out[at : at + size, lane : lane + 128] = block.astype(BF16)


def per_device(
    grad_gate,
    grad_up,
    grad_down,
    proj_gate,
    proj_up,
    proj_down,
    first_gate,
    second_gate,
    first_up,
    second_up,
    first_down,
    second_down,
):
    gate, up, down = grad_gate.T, grad_up.T, grad_down.T
    run = Chain()
    half, piece = pltpu.VMEM((32, 6400), BF16), pltpu.VMEM((16, 6400), BF16)
    part, held = pltpu.VMEM((192, 320), BF16), pltpu.VMEM((320, 3200), BF16)
    row, pair_row = pltpu.VMEM((2, 1600), F32), pltpu.VMEM((4, 3200), F32)
    whole = jax.ShapeDtypeStruct((320, 3200), BF16)
    state, down_state = jax.ShapeDtypeStruct((16, 3200), F32), jax.ShapeDtypeStruct((32, 1600), F32)

    forth, back, rest_g, rest_u, gate, up = run(
        first_kernel,
        (half, half, part, part, held, held),
        proj_gate.T, gate, proj_up.T, up,
        in_specs=(HBM,) * 4,
        scratch=(pltpu.VMEM((2, 320, 256), BF16), pltpu.SemaphoreType.DMA((12,))),
    )
    from_below, from_above = ring_send(forth, 1, 0), ring_send(back, 3, 0)
    forth, back, near, far, keep = run(
        rest_kernel, (half, half, half, half, pltpu.VMEM((64, 6400), BF16)), rest_g, gate, rest_u, up
    )
    high_below, low_above = ring_send(forth, 1, 0), ring_send(back, 3, 0)

    own_down, other_down = run(down_kernel, (pltpu.VMEM((128, 1600), BF16),) * 2, proj_down, down)
    other_down = core_send(other_down)

    forth, back = run(pass_kernel, (half, half), near, from_below, far, from_above)
    low_below, high_above = ring_send(forth, 1, 0), ring_send(back, 3, 0)

    own_down, other_down = run(
        down_split_kernel, (pltpu.VMEM((64, 1600), F32), pltpu.VMEM((64, 1600), BF16)), own_down, other_down
    )
    other_down = z_swap(other_down, False)
    own_down, other_down = run(
        down_halve_kernel, (pltpu.VMEM((32, 1600), F32), pltpu.VMEM((32, 1600), BF16)), own_down, other_down
    )
    other_down = z_swap(other_down, True)
    sums_d, total_d = run(
        down_sum_kernel, (row, pltpu.VMEM((32, 1600), F32)), own_down, other_down, first_down, second_down
    )
    other_d = core_send(sums_d)

    opposite, above, below, own = run(
        gather_kernel,
        (piece, piece, piece, pltpu.VMEM((16, 6400), F32)),
        keep, low_above, low_below, high_below, high_above,
    )
    opposite, above, below = ring_send(opposite, 2, 1), ring_send(above, 1, 1), ring_send(below, 3, 1)

    (sums_d,) = run(add_kernel, (row,), sums_d, other_d)
    other_d = z_swap(sums_d, False)

    states = (first_gate, second_gate, first_up, second_up)
    sums, total = run(
        pair_sum_kernel, (pair_row, pltpu.VMEM((16, 6400), F32)), own, opposite, above, below, *states
    )
    sums_one = (sums, ring_send(sums, 2, 1), ring_send(sums, 1, 1), ring_send(sums, 3, 1))
    (sums_d,) = run(add_kernel, (row,), sums_d, other_d)
    other_d = z_swap(sums_d, True)
    first_gate_new, second_gate_new, first_up_new, second_up_new = run(
        pair_moment_kernel, (state, state, state, state), total, *states
    )
    (sums,) = run(add_kernel, (pair_row,), *sums_one)
    sums_two = (sums, ring_send(sums, 2, 0), ring_send(sums, 1, 0), ring_send(sums, 3, 0))
    (update_down,) = run(
        down_update_kernel,
        (jax.ShapeDtypeStruct((1600, 640), BF16),),
        down, sums_d, other_d,
        scratch=(pltpu.VMEM((1, 1664), F32),),
    )
    first_down_new, second_down_new = run(
        down_moment_kernel, (down_state, down_state), total_d, first_down, second_down
    )
    update_gate, update_up = run(
        update_kernel,
        (whole, whole),
        gate, up, *sums_two,
        out_specs=(HBM, HBM),
        scratch=(held, held, pltpu.SemaphoreType.DMA((10,))),
    )
    return (
        update_gate.T,
        update_up.T,
        update_down.T,
        first_gate_new,
        second_gate_new,
        first_up_new,
        second_up_new,
        first_down_new,
        second_down_new,
    )


def solution(mesh):
    fine = Mesh(mesh.devices.reshape(SIZES), AXES)
    gradient, state = P(ACROSS, ALONG), P(ALONG, ACROSS)
    return jax.shard_map(
        per_device,
        mesh=fine,
        in_specs=(
            gradient,
            gradient,
            gradient,
            P(None, ALONG),
            P(None, ALONG),
            P(None, ACROSS),
            state,
            state,
            state,
            state,
            gradient,
            gradient,
        ),
        out_specs=(
            gradient,
            gradient,
            gradient,
            state,
            state,
            state,
            state,
            gradient,
            gradient,
        ),
        check_vma=False,
    )
```

```python
import jax
import jax.numpy as jnp
from jax import lax
from jax.experimental import pallas as pl
from jax.experimental.pallas import tpu as pltpu
from jax.sharding import Mesh
from jax.sharding import PartitionSpec as P

STEP = 100

beta_first = 0.9
beta_second = 0.999
adam_epsilon = 1e-08
norm_epsilon = 1e-06
update_scale = 4.0

AXES = ("y", "x", "z", "core")
SIZES = (4, 4, 4, 2)
ALONG = ("y", "x")
ACROSS = ("z", "core")
F32 = jnp.float32
BF16 = jnp.bfloat16


def device_number(y, x, z, core):
    return ((y * 4 + x) * 4 + z) * 2 + core


def ring_pairs(shift, stage):
    pairs = []
    for y in range(4):
        for x in range(4):
            for z in range(4):
                for core in range(2):
                    source = device_number(y, x, z, core)
                    if (core == 0) == (stage == 0):
                        target = device_number(y, (x + shift) % 4, z, core)
                    else:
                        target = device_number((y + shift) % 4, x, z, core)
                    pairs.append((source, target))
    return pairs


def ring_send(value, shift, stage):
    return lax.ppermute(value, AXES, ring_pairs(shift, stage))


def z_swap(value, far):
    pairs = [(0, 3), (3, 0), (1, 2), (2, 1)] if far else [(0, 1), (1, 0), (2, 3), (3, 2)]
    return lax.ppermute(value, "z", pairs)


def core_send(value):
    return lax.ppermute(value, "core", [(0, 1), (1, 0)])


VMEM = pl.BlockSpec(memory_space=pltpu.VMEM)
HBM = pl.BlockSpec(memory_space=pltpu.HBM)


class Chain:
    def __init__(self):
        self.last = None

    def __call__(self, body, outs, *operands, in_specs=None, out_specs=None, scratch=(), limit=8):
        specs = [VMEM] * len(operands) if in_specs is None else list(in_specs)
        count, made = len(operands), len(outs)
        if self.last is not None:
            operands = operands + (self.last,)
            specs.append(VMEM)
        operands = [
            pltpu.with_memory_space_constraint(operand, spec.memory_space)
            for operand, spec in zip(operands, specs)
        ]

        def kernel(*refs):
            refs, token = refs[: len(operands)], refs[len(operands) :]
            token, rest = token[made], token[:made] + token[made + 1 :]
            token[...] = jnp.zeros_like(token)
            body(*refs[:count], *rest)

        *result, self.last = pl.pallas_call(
            kernel,
            name=body.__name__,
            out_shape=[*outs, pltpu.VMEM((8, 128), F32)],
            in_specs=specs,
            out_specs=[*([VMEM] * made if out_specs is None else out_specs), VMEM],
            scratch_shapes=scratch,
            compiler_params=pltpu.CompilerParams(vmem_limit_bytes=limit * 2**20),
            cost_estimate=pl.CostEstimate(flops=0, bytes_accessed=0, transcendentals=0),
        )(*operands)
        return result


def wide(*terms):
    total = terms[0].astype(F32)
    for term in terms[1:]:
        total = total + term.astype(F32)
    return total


def picked(rows, projection, contract):
    place = lax.broadcasted_iota(jnp.int32, (256, 256), 1)
    chosen = jnp.where(rows == place, 1.0, 0.0).astype(BF16)
    return lax.dot_general(chosen, projection, (((1,), (contract,)), ((), ())), preferred_element_type=F32).astype(BF16)


def fsdp_rows():
    y, x, core = lax.axis_index("y"), lax.axis_index("x"), lax.axis_index("core")
    step = lax.broadcasted_iota(jnp.int32, (256, 1), 0)
    outer, inner = step // 64, step // 16 % 4
    outer = jnp.where(outer == 0, 2, jnp.where(outer == 3, 0, jnp.where(outer == 1, 1, 3)))
    inner = jnp.where(inner == 1, 2, jnp.where(inner == 2, 1, inner))
    on_x, on_y = jnp.where(core == 0, outer, inner), jnp.where(core == 0, inner, outer)
    return ((y + on_y) % 4 * 4 + (x + on_x) % 4) * 16 + step % 16


def row_rows():
    z, core = lax.axis_index("z"), lax.axis_index("core")
    step = lax.broadcasted_iota(jnp.int32, (256, 1), 0)
    turn = step // 32 % 4
    to = jnp.where(turn % 2 == 0, z, 3 - z)
    to = jnp.where(turn < 2, to, to + 1 - to % 2 * 2)
    return (to * 2 + (core + step // 128) % 2) * 32 + step % 32


PARTS = tuple(range(0, 3200, 640))


def first_kernel(gate_proj, gate, up_proj, up, forth, back, gate_rest, up_rest, gate_kept, up_kept, projs, sems):
    copies = [
        pltpu.make_async_copy(source, target, sems.at[index])
        for index, (source, target) in enumerate(
            ((gate_proj, projs.at[0]), (up_proj, projs.at[1]), (gate, gate_kept), (up, up_kept))
        )
    ]
    for copy in copies:
        copy.start()
    rows = fsdp_rows()
    ordered = []
    for index, rest in enumerate((gate_rest, up_rest)):
        copies[index].wait()
        ordered.append(picked(rows, projs[index], 1))
        rest[...] = ordered[index][64:]
    for index, kept in enumerate((gate_kept, up_kept)):
        copies[2 + index].wait()
        for at in range(0, 3200, 640):
            part = jnp.dot(ordered[index][:64], kept[:, at : at + 640], preferred_element_type=F32).astype(BF16)
            base = index * 3200 + at
            forth[:, base : base + 640] = part[:32]
            back[:, base : base + 640] = part[32:]


def rest_kernel(gate_rest, gate, up_rest, up, forth, back, near, far, keep):
    for rest, grad, base in ((gate_rest, gate, 0), (up_rest, up, 3200)):
        for at in range(0, 3200, 640):
            to = slice(base + at, base + at + 640)
            part = jnp.dot(rest[...], grad[:, at : at + 640], preferred_element_type=F32).astype(BF16)
            near[:, to] = part[:32]
            forth[:, to] = part[32:64]
            back[:, to] = part[64:96]
            far[:, to] = part[96:128]
            keep[:, to] = part[128:]


def pass_kernel(near, from_below, far, from_above, onward, backward):
    onward[...] = wide(near[...], from_below[...]).astype(BF16)
    backward[...] = wide(far[...], from_above[...]).astype(BF16)


def collect_kernel(keep, low_above, high_below, low, high):
    low[...] = wide(keep[:32], low_above[...])
    high[...] = wide(keep[32:], high_below[...])


def near_kernel(low, low_below, own, opposite):
    total = wide(low[...], low_below[...])
    own[...] = total[:16]
    opposite[...] = total[16:].astype(BF16)


def far_kernel(high, high_above, above, below):
    total = wide(high[...], high_above[...]).astype(BF16)
    above[...] = total[:16]
    below[...] = total[16:]


def moments(projected, first, second):
    return (
        beta_first * first[...] + (1.0 - beta_first) * projected,
        beta_second * second[...] + (1.0 - beta_second) * projected * projected,
    )


def channel_sums(projected, first, second):
    first_value, second_value = moments(projected, first, second)
    corrected = (
        first_value
        / (1.0 - beta_first**STEP)
        / (jnp.sqrt(second_value / (1.0 - beta_second**STEP)) + adam_epsilon)
    )
    return jnp.sum(corrected * corrected, 0, keepdims=True), jnp.sum(projected * projected, 0, keepdims=True)


def pair_sum_kernel(own, a, b, first_gate, second_gate, first_up, second_up, sums, total):
    projected = wide(own[...], a[...], b[...])
    total[...] = projected
    sums[0:1], sums[1:2] = channel_sums(projected[:, :3200], first_gate, second_gate)
    sums[2:3], sums[3:4] = channel_sums(projected[:, 3200:], first_up, second_up)


def pair_moment_kernel(total, first_gate, second_gate, first_up, second_up, *news):
    news[0][...], news[1][...] = moments(total[:, :3200], first_gate, second_gate)
    news[2][...], news[3][...] = moments(total[:, 3200:], first_up, second_up)


def down_sum_kernel(own, other, first, second, sums, total):
    projected = wide(own[...], other[...])
    total[...] = projected
    sums[...] = jnp.zeros_like(sums)
    sums[0:1], sums[1:2] = channel_sums(projected, first, second)


def down_moment_kernel(total, first, second, *news):
    news[0][...], news[1][...] = moments(total[...], first, second)


def add_kernel(*refs):
    refs[-1][...] = wide(*(ref[...] for ref in refs[:-1]))


def scale_of(corrected_sq, projected_sq):
    return update_scale * (jnp.sqrt(corrected_sq) / (jnp.sqrt(projected_sq) + norm_epsilon))


def update_kernel(gate, up, a, b, c, d, gate_out, up_out, gate_made, up_made, sems):
    sums = wide(a[...], b[...], c[...], d[...])
    copies = []
    for index, (grad, made, out) in enumerate(((gate, gate_made, gate_out), (up, up_made, up_out))):
        scale = scale_of(sums[2 * index : 2 * index + 1], sums[2 * index + 1 : 2 * index + 2])
        for at in range(0, 320, 64):
            made[at : at + 64] = (grad[at : at + 64].astype(F32) * scale).astype(BF16)
        copies.append(pltpu.make_async_copy(made, out, sems.at[index]))
        copies[-1].start()
    for copy in copies:
        copy.wait()


def down_kernel(proj, grad, own, other):
    ordered = picked(row_rows(), proj[...], 0)
    for at, size in ((0, 512), (512, 512), (1024, 576)):
        part = lax.dot_general(
            ordered, grad[at : at + size], (((1,), (1,)), ((), ())), preferred_element_type=F32
        ).astype(BF16)
        own[:, at : at + size] = part[:128]
        other[:, at : at + size] = part[128:]


def down_split_kernel(own, other, keep, send):
    total = wide(own[...], other[...])
    keep[...] = total[:64]
    send[...] = total[64:].astype(BF16)


def down_halve_kernel(own, other, keep, send):
    total = wide(own[...], other[...])
    keep[...] = total[:32]
    send[...] = total[32:].astype(BF16)


def down_update_kernel(grad, own, other, out, scale):
    sums = wide(own[...], other[...])
    scale[:, :1600] = scale_of(sums[0:1], sums[1:2])
    for at in range(0, 1600, 128):
        size = min(128, 1600 - at)
        column = jnp.broadcast_to(scale[:, at : at + 128], (128, 128)).T[:size]
        for lane in range(0, 640, 128):
            block = grad[at : at + size, lane : lane + 128].astype(F32) * column
            out[at : at + size, lane : lane + 128] = block.astype(BF16)


def per_device(
    grad_gate,
    grad_up,
    grad_down,
    proj_gate,
    proj_up,
    proj_down,
    first_gate,
    second_gate,
    first_up,
    second_up,
    first_down,
    second_down,
):
    gate, up, down = grad_gate.T, grad_up.T, grad_down.T
    run = Chain()
    half, piece = pltpu.VMEM((32, 6400), BF16), pltpu.VMEM((16, 6400), BF16)
    part, held = pltpu.VMEM((192, 320), BF16), pltpu.VMEM((320, 3200), BF16)
    row, pair_row = pltpu.VMEM((8, 1600), F32), pltpu.VMEM((4, 3200), F32)
    whole = jax.ShapeDtypeStruct((320, 3200), BF16)
    state, down_state = jax.ShapeDtypeStruct((16, 3200), F32), jax.ShapeDtypeStruct((32, 1600), F32)

    forth, back, rest_g, rest_u, gate, up = run(
        first_kernel,
        (half, half, part, part, held, held),
        proj_gate.T, gate, proj_up.T, up,
        in_specs=(HBM,) * 4,
        scratch=(pltpu.VMEM((2, 320, 256), BF16), pltpu.SemaphoreType.DMA((4,))),
    )
    from_below, from_above = ring_send(forth, 1, 0), ring_send(back, 3, 0)
    own_down, other_down = run(down_kernel, (pltpu.VMEM((128, 1600), BF16),) * 2, proj_down, down)
    other_down = core_send(other_down)
    forth, back, near, far, keep = run(
        rest_kernel, (half, half, half, half, pltpu.VMEM((64, 6400), BF16)), rest_g, gate, rest_u, up
    )
    high_below, low_above = ring_send(forth, 1, 0), ring_send(back, 3, 0)
    forth, back = run(pass_kernel, (half, half), near, from_below, far, from_above)
    low_below, high_above = ring_send(forth, 1, 0), ring_send(back, 3, 0)
    own_down, other_down = run(
        down_split_kernel, (pltpu.VMEM((64, 1600), F32), pltpu.VMEM((64, 1600), BF16)), own_down, other_down
    )
    other_down = z_swap(other_down, False)
    low, high = run(collect_kernel, (pltpu.VMEM((32, 6400), F32),) * 2, keep, low_above, high_below)

    own, opposite = run(near_kernel, (pltpu.VMEM((16, 6400), F32), piece), low, low_below)
    opposite = ring_send(opposite, 2, 1)
    above, below = run(far_kernel, (piece, piece), high, high_above)
    above, below = ring_send(above, 1, 1), ring_send(below, 3, 1)
    own_down, other_down = run(
        down_halve_kernel, (pltpu.VMEM((32, 1600), F32), pltpu.VMEM((32, 1600), BF16)), own_down, other_down
    )
    other_down = z_swap(other_down, True)

    states = (first_gate, second_gate, first_up, second_up)
    (own,) = run(add_kernel, (pltpu.VMEM((16, 6400), F32),), own, opposite)
    sums, total = run(
        pair_sum_kernel, (pair_row, pltpu.VMEM((16, 6400), F32)), own, above, below, *states
    )
    sums_one = (sums, ring_send(sums, 2, 1), ring_send(sums, 1, 1), ring_send(sums, 3, 1))
    sums_d, total_d = run(
        down_sum_kernel, (row, pltpu.VMEM((32, 1600), F32)), own_down, other_down, first_down, second_down
    )
    other_d = z_swap(sums_d, False)
    first_gate_new, second_gate_new, first_up_new, second_up_new = run(
        pair_moment_kernel, (state, state, state, state), total, *states
    )
    (sums,) = run(add_kernel, (pair_row,), *sums_one)
    sums_two = (sums, ring_send(sums, 2, 0), ring_send(sums, 1, 0), ring_send(sums, 3, 0))
    (sums_d,) = run(add_kernel, (row,), sums_d, other_d)
    other_d = z_swap(sums_d, True)
    first_down_new, second_down_new = run(
        down_moment_kernel, (down_state, down_state), total_d, first_down, second_down
    )
    update_gate, update_up = run(
        update_kernel,
        (whole, whole),
        gate, up, *sums_two,
        out_specs=(HBM, HBM),
        scratch=(held, held, pltpu.SemaphoreType.DMA((2,))),
    )
    (sums_d,) = run(add_kernel, (row,), sums_d, other_d)
    other_d = core_send(sums_d)
    (update_down,) = run(
        down_update_kernel,
        (jax.ShapeDtypeStruct((1600, 640), BF16),),
        down, sums_d, other_d,
        scratch=(pltpu.VMEM((1, 1664), F32),),
    )
    return (
        update_gate.T,
        update_up.T,
        update_down.T,
        first_gate_new,
        second_gate_new,
        first_up_new,
        second_up_new,
        first_down_new,
        second_down_new,
    )


def solution(mesh):
    fine = Mesh(mesh.devices.reshape(SIZES), AXES)
    gradient, state = P(ACROSS, ALONG), P(ALONG, ACROSS)
    return jax.shard_map(
        per_device,
        mesh=fine,
        in_specs=(
            gradient,
            gradient,
            gradient,
            P(None, ALONG),
            P(None, ALONG),
            P(None, ACROSS),
            state,
            state,
            state,
            state,
            gradient,
            gradient,
        ),
        out_specs=(
            gradient,
            gradient,
            gradient,
            state,
            state,
            state,
            state,
            gradient,
            gradient,
        ),
        check_vma=False,
    )
```

```python
import jax
import jax.numpy as jnp
from jax import lax
from jax.experimental import pallas as pl
from jax.experimental.pallas import tpu as pltpu
from jax.sharding import Mesh
from jax.sharding import PartitionSpec as P

STEP = 100

beta_first = 0.9
beta_second = 0.999
adam_epsilon = 1e-08
norm_epsilon = 1e-06
update_scale = 4.0

AXES = ("y", "x", "z", "core")
SIZES = (4, 4, 4, 2)
ALONG = ("y", "x")
ACROSS = ("z", "core")
F32 = jnp.float32
BF16 = jnp.bfloat16


def device_number(y, x, z, core):
    return ((y * 4 + x) * 4 + z) * 2 + core


def ring_pairs(shift, stage):
    pairs = []
    for y in range(4):
        for x in range(4):
            for z in range(4):
                for core in range(2):
                    source = device_number(y, x, z, core)
                    if (core == 0) == (stage == 0):
                        target = device_number(y, (x + shift) % 4, z, core)
                    else:
                        target = device_number((y + shift) % 4, x, z, core)
                    pairs.append((source, target))
    return pairs


def ring_send(value, shift, stage):
    return lax.ppermute(value, AXES, ring_pairs(shift, stage))


def ring_swap(value, far, stage):
    pairs = []
    for y in range(4):
        for x in range(4):
            for z in range(4):
                for core in range(2):
                    source = device_number(y, x, z, core)
                    if (core == 0) == (stage == 0):
                        target = device_number(y, 3 - x if far else x ^ 1, z, core)
                    else:
                        target = device_number(3 - y if far else y ^ 1, x, z, core)
                    pairs.append((source, target))
    return lax.ppermute(value, AXES, pairs)


def z_swap(value, far):
    pairs = [(0, 3), (3, 0), (1, 2), (2, 1)] if far else [(0, 1), (1, 0), (2, 3), (3, 2)]
    return lax.ppermute(value, "z", pairs)


def core_send(value):
    return lax.ppermute(value, "core", [(0, 1), (1, 0)])


VMEM = pl.BlockSpec(memory_space=pltpu.VMEM)
HBM = pl.BlockSpec(memory_space=pltpu.HBM)


class Chain:
    def __init__(self):
        self.last = None

    def __call__(self, body, outs, *operands, in_specs=None, out_specs=None, scratch=(), limit=8):
        specs = [VMEM] * len(operands) if in_specs is None else list(in_specs)
        count, made = len(operands), len(outs)
        if self.last is not None:
            operands = operands + (self.last,)
            specs.append(VMEM)
        operands = [
            pltpu.with_memory_space_constraint(operand, spec.memory_space)
            for operand, spec in zip(operands, specs)
        ]

        def kernel(*refs):
            refs, token = refs[: len(operands)], refs[len(operands) :]
            token, rest = token[made], token[:made] + token[made + 1 :]
            token[...] = jnp.zeros_like(token)
            body(*refs[:count], *rest)

        *result, self.last = pl.pallas_call(
            kernel,
            name=body.__name__,
            out_shape=[*outs, pltpu.VMEM((8, 128), F32)],
            in_specs=specs,
            out_specs=[*([VMEM] * made if out_specs is None else out_specs), VMEM],
            scratch_shapes=scratch,
            compiler_params=pltpu.CompilerParams(vmem_limit_bytes=limit * 2**20),
            cost_estimate=pl.CostEstimate(flops=0, bytes_accessed=0, transcendentals=0),
        )(*operands)
        return result


def wide(*terms):
    total = terms[0].astype(F32)
    for term in terms[1:]:
        total = total + term.astype(F32)
    return total


def picked(rows, projection, contract):
    place = lax.broadcasted_iota(jnp.int32, (256, 256), 1)
    chosen = jnp.where(rows == place, 1.0, 0.0).astype(BF16)
    return lax.dot_general(chosen, projection, (((1,), (contract,)), ((), ())), preferred_element_type=F32).astype(BF16)


def fsdp_rows():
    y, x, core = lax.axis_index("y"), lax.axis_index("x"), lax.axis_index("core")
    step = lax.broadcasted_iota(jnp.int32, (256, 1), 0)
    outer, inner = step // 64, step // 16 % 4
    outer = jnp.where(outer == 0, 2, jnp.where(outer == 3, 0, jnp.where(outer == 1, 1, 3)))
    inner = jnp.where(inner == 1, 2, jnp.where(inner == 2, 1, inner))
    on_x, on_y = jnp.where(core == 0, outer, inner), jnp.where(core == 0, inner, outer)
    return ((y + on_y) % 4 * 4 + (x + on_x) % 4) * 16 + step % 16


def row_rows():
    z, core = lax.axis_index("z"), lax.axis_index("core")
    step = lax.broadcasted_iota(jnp.int32, (256, 1), 0)
    turn = step // 32 % 4
    to = jnp.where(turn % 2 == 0, z, 3 - z)
    to = jnp.where(turn < 2, to, to + 1 - to % 2 * 2)
    return (to * 2 + (core + step // 128) % 2) * 32 + step % 32


PARTS = tuple(range(0, 3200, 640))


def first_kernel(gate_proj, gate, up_proj, up, forth, back, gate_rest, up_rest, gate_kept, up_kept, projs, sems):
    proj_copies = [
        pltpu.make_async_copy(source, projs.at[index], sems.at[index]) for index, source in enumerate((gate_proj, up_proj))
    ]
    parts = ((0, 0, 1664), (0, 1664, 1536), (1, 0, 1664), (1, 1664, 1536))
    copies = []
    for number, (index, at, size) in enumerate(parts):
        source, target = ((gate, gate_kept), (up, up_kept))[index]
        to = pl.ds(at, size)
        copies.append(pltpu.make_async_copy(source.at[:, to], target.at[:, to], sems.at[2 + number]))
    for copy in proj_copies + copies:
        copy.start()
    rows = fsdp_rows()
    ordered = []
    for index, rest in enumerate((gate_rest, up_rest)):
        proj_copies[index].wait()
        ordered.append(picked(rows, projs[index], 1))
        rest[...] = ordered[index][64:]
    for copy, (index, start, size) in zip(copies, parts):
        copy.wait()
        kept = (gate_kept, up_kept)[index]
        for at in range(start, start + size, 512):
            width = min(512, start + size - at)
            part = jnp.dot(ordered[index][:64], kept[:, at : at + width], preferred_element_type=F32).astype(BF16)
            base = index * 3200 + at
            forth[:, base : base + width] = part[:32]
            back[:, base : base + width] = part[32:]


def rest_kernel(gate_rest, gate, up_rest, up, forth, back, near, far, keep):
    for rest, grad, base in ((gate_rest, gate, 0), (up_rest, up, 3200)):
        for at in range(0, 3200, 640):
            to = slice(base + at, base + at + 640)
            part = jnp.dot(rest[...], grad[:, at : at + 640], preferred_element_type=F32).astype(BF16)
            near[:, to] = part[:32]
            forth[:, to] = part[32:64]
            back[:, to] = part[64:96]
            far[:, to] = part[96:128]
            keep[:, to] = part[128:]


def pass_kernel(near, from_below, far, from_above, onward, backward):
    onward[...] = wide(near[...], from_below[...]).astype(BF16)
    backward[...] = wide(far[...], from_above[...]).astype(BF16)


def collect_kernel(keep, high_below, low_above, low, high):
    low[...] = wide(keep[:32], low_above[...])
    high[...] = wide(keep[32:], high_below[...])


def near_kernel(low, low_below, own, opposite):
    total = wide(low[...], low_below[...])
    own[...] = total[:16]
    opposite[...] = total[16:].astype(BF16)


def far_kernel(high, high_above, above, below):
    total = wide(high[...], high_above[...]).astype(BF16)
    above[...] = total[:16]
    below[...] = total[16:]


def moments(projected, first, second):
    return (
        beta_first * first[...] + (1.0 - beta_first) * projected,
        beta_second * second[...] + (1.0 - beta_second) * projected * projected,
    )


def channel_sums(projected, first, second):
    first_value, second_value = moments(projected, first, second)
    corrected = (
        first_value
        / (1.0 - beta_first**STEP)
        / (jnp.sqrt(second_value / (1.0 - beta_second**STEP)) + adam_epsilon)
    )
    return jnp.sum(corrected * corrected, 0, keepdims=True), jnp.sum(projected * projected, 0, keepdims=True)


def pair_sum_kernel(own, a, b, first_gate, second_gate, first_up, second_up, sums, sent, total):
    projected = wide(own[...], a[...], b[...])
    total[...] = projected
    sums[0:1], sums[1:2] = channel_sums(projected[:, :3200], first_gate, second_gate)
    sums[2:3], sums[3:4] = channel_sums(projected[:, 3200:], first_up, second_up)
    sent[...] = sums[...].astype(BF16)


def moment_kernel(total, total_d, first_gate, second_gate, first_up, second_up, first_down, second_down, *news):
    news[0][...], news[1][...] = moments(total[:, :3200], first_gate, second_gate)
    news[2][...], news[3][...] = moments(total[:, 3200:], first_up, second_up)
    news[4][...], news[5][...] = moments(total_d[...], first_down, second_down)


def down_sum_kernel(own, other, first, second, sums, sent, total):
    projected = wide(own[...], other[...])
    total[...] = projected
    sums[...] = jnp.zeros_like(sums)
    sums[0:1], sums[1:2] = channel_sums(projected, first, second)
    sent[...] = sums[...].astype(BF16)


def add_kernel(*refs):
    refs[-1][...] = wide(*(ref[...] for ref in refs[:-1]))


def sum_kernel(*refs):
    total = wide(*(ref[...] for ref in refs[:-2]))
    refs[-2][...] = total
    refs[-1][...] = total.astype(BF16)


def scale_of(corrected_sq, projected_sq):
    return update_scale * (jnp.sqrt(corrected_sq) / (jnp.sqrt(projected_sq) + norm_epsilon))


def scale_kernel(own, other, scale):
    sums = wide(own[...], other[...])
    scale[0:1] = scale_of(sums[0:1], sums[1:2])
    scale[1:2] = scale_of(sums[2:3], sums[3:4])


def update_kernel(gate, up, scale, gate_out, up_out, gate_made, up_made, sems):
    copies = []
    for index, (grad, made, out) in enumerate(((gate, gate_made, gate_out), (up, up_made, up_out))):
        made[...] = (grad[...].astype(F32) * scale[index : index + 1]).astype(BF16)
        copies.append(pltpu.make_async_copy(made, out, sems.at[index]))
        copies[-1].start()
    for copy in copies:
        copy.wait()


def down_kernel(proj, grad, own, other):
    ordered = picked(row_rows(), proj[...], 0)
    for at, size in ((0, 512), (512, 512), (1024, 576)):
        part = lax.dot_general(
            ordered, grad[at : at + size], (((1,), (1,)), ((), ())), preferred_element_type=F32
        ).astype(BF16)
        own[:, at : at + size] = part[:128]
        other[:, at : at + size] = part[128:]


def down_split_kernel(own, other, keep, send):
    total = wide(own[...], other[...])
    keep[...] = total[:64]
    send[...] = total[64:].astype(BF16)


def down_halve_kernel(own, other, keep, send):
    total = wide(own[...], other[...])
    keep[...] = total[:32]
    send[...] = total[32:].astype(BF16)


def down_update_kernel(grad, own, other, out, scale):
    sums = wide(own[...], other[...])
    scale[:, :1600] = scale_of(sums[0:1], sums[1:2])
    for at in range(0, 1600, 128):
        size = min(128, 1600 - at)
        column = jnp.broadcast_to(scale[:, at : at + 128], (128, 128)).T[:size]
        for lane in range(0, 640, 128):
            block = grad[at : at + size, lane : lane + 128].astype(F32) * column
            out[at : at + size, lane : lane + 128] = block.astype(BF16)


def per_device(
    grad_gate,
    grad_up,
    grad_down,
    proj_gate,
    proj_up,
    proj_down,
    first_gate,
    second_gate,
    first_up,
    second_up,
    first_down,
    second_down,
):
    gate, up, down = grad_gate.T, grad_up.T, grad_down.T
    run = Chain()
    half, piece = pltpu.VMEM((32, 6400), BF16), pltpu.VMEM((16, 6400), BF16)
    part, held = pltpu.VMEM((192, 320), BF16), pltpu.VMEM((320, 3200), BF16)
    row, pair_row = pltpu.VMEM((8, 1600), F32), pltpu.VMEM((4, 3200), F32)
    sent_row, sent_pair = pltpu.VMEM((8, 1600), BF16), pltpu.VMEM((4, 3200), BF16)
    whole = jax.ShapeDtypeStruct((320, 3200), BF16)
    state, down_state = jax.ShapeDtypeStruct((16, 3200), F32), jax.ShapeDtypeStruct((32, 1600), F32)

    forth, back, rest_g, rest_u, gate, up = run(
        first_kernel,
        (half, half, part, part, held, held),
        proj_gate.T, gate, proj_up.T, up,
        in_specs=(HBM,) * 4,
        scratch=(pltpu.VMEM((2, 320, 256), BF16), pltpu.SemaphoreType.DMA((6,))),
    )
    from_below, from_above = ring_send(forth, 1, 0), ring_send(back, 3, 0)
    forth, back, near, far, keep = run(
        rest_kernel, (half, half, half, half, pltpu.VMEM((64, 6400), BF16)), rest_g, gate, rest_u, up
    )
    high_below, low_above = ring_send(forth, 1, 0), ring_send(back, 3, 0)
    own_down, other_down = run(down_kernel, (pltpu.VMEM((128, 1600), BF16),) * 2, proj_down, down)
    other_down = core_send(other_down)
    forth, back = run(pass_kernel, (half, half), near, from_below, far, from_above)
    low_below, high_above = ring_send(forth, 1, 0), ring_send(back, 3, 0)
    low, high = run(collect_kernel, (pltpu.VMEM((32, 6400), F32),) * 2, keep, high_below, low_above)
    own_down, other_down = run(
        down_split_kernel, (pltpu.VMEM((64, 1600), F32), pltpu.VMEM((64, 1600), BF16)), own_down, other_down
    )
    other_down = z_swap(other_down, False)

    own, opposite = run(near_kernel, (pltpu.VMEM((16, 6400), F32), piece), low, low_below)
    opposite = ring_send(opposite, 2, 1)
    above, below = run(far_kernel, (piece, piece), high, high_above)
    above, below = ring_send(above, 1, 1), ring_send(below, 3, 1)
    own_down, other_down = run(
        down_halve_kernel, (pltpu.VMEM((32, 1600), F32), pltpu.VMEM((32, 1600), BF16)), own_down, other_down
    )
    other_down = z_swap(other_down, True)

    states = (first_gate, second_gate, first_up, second_up)
    (own,) = run(add_kernel, (pltpu.VMEM((16, 6400), F32),), own, opposite)
    sums, sent, total = run(
        pair_sum_kernel, (pair_row, sent_pair, pltpu.VMEM((16, 6400), F32)), own, above, below, *states
    )
    other = ring_swap(sent, False, 1)
    sums_d, sent_d, total_d = run(
        down_sum_kernel, (row, sent_row, pltpu.VMEM((32, 1600), F32)), own_down, other_down, first_down, second_down
    )
    other_d = z_swap(sent_d, False)
    sums, sent = run(sum_kernel, (pair_row, sent_pair), sums, other)
    other = ring_swap(sent, True, 1)
    sums_d, sent_d = run(sum_kernel, (row, sent_row), sums_d, other_d)
    other_d = z_swap(sent_d, True)
    sums, sent = run(sum_kernel, (pair_row, sent_pair), sums, other)
    other = ring_swap(sent, False, 0)
    sums_d, sent_d = run(sum_kernel, (row, sent_row), sums_d, other_d)
    other_d = core_send(sent_d)
    news = run(moment_kernel, (state,) * 4 + (down_state,) * 2, total, total_d, *states, first_down, second_down)
    sums, sent = run(sum_kernel, (pair_row, sent_pair), sums, other)
    other = ring_swap(sent, True, 0)
    (update_down,) = run(
        down_update_kernel,
        (jax.ShapeDtypeStruct((1600, 640), BF16),),
        down, sums_d, other_d,
        scratch=(pltpu.VMEM((1, 1664), F32),),
    )
    (scale,) = run(scale_kernel, (pltpu.VMEM((2, 3200), F32),), sums, other)
    update_gate, update_up = run(
        update_kernel,
        (whole, whole),
        gate, up, scale,
        out_specs=(HBM, HBM),
        scratch=(held, held, pltpu.SemaphoreType.DMA((2,))),
    )
    return (
        update_gate.T,
        update_up.T,
        update_down.T,
        *news,
    )


def solution(mesh):
    fine = Mesh(mesh.devices.reshape(SIZES), AXES)
    gradient, state = P(ACROSS, ALONG), P(ALONG, ACROSS)
    return jax.shard_map(
        per_device,
        mesh=fine,
        in_specs=(
            gradient,
            gradient,
            gradient,
            P(None, ALONG),
            P(None, ALONG),
            P(None, ACROSS),
            state,
            state,
            state,
            state,
            gradient,
            gradient,
        ),
        out_specs=(
            gradient,
            gradient,
            gradient,
            state,
            state,
            state,
            state,
            gradient,
            gradient,
        ),
        check_vma=False,
    )
```

```python
import jax
import jax.numpy as jnp
from jax import lax
from jax.experimental import pallas as pl
from jax.experimental.pallas import tpu as pltpu
from jax.sharding import Mesh
from jax.sharding import PartitionSpec as P

STEP = 100

beta_first = 0.9
beta_second = 0.999
adam_epsilon = 1e-08
norm_epsilon = 1e-06
update_scale = 4.0

AXES = ("y", "x", "z", "core")
SIZES = (4, 4, 4, 2)
ALONG = ("y", "x")
ACROSS = ("z", "core")
F32 = jnp.float32
BF16 = jnp.bfloat16


def device_number(y, x, z, core):
    return ((y * 4 + x) * 4 + z) * 2 + core


def ring_pairs(shift, stage):
    pairs = []
    for y in range(4):
        for x in range(4):
            for z in range(4):
                for core in range(2):
                    source = device_number(y, x, z, core)
                    if (core == 0) == (stage == 0):
                        target = device_number(y, (x + shift) % 4, z, core)
                    else:
                        target = device_number((y + shift) % 4, x, z, core)
                    pairs.append((source, target))
    return pairs


def ring_send(value, shift, stage):
    return lax.ppermute(value, AXES, ring_pairs(shift, stage))


def ring_swap(value, far, stage):
    pairs = []
    for y in range(4):
        for x in range(4):
            for z in range(4):
                for core in range(2):
                    source = device_number(y, x, z, core)
                    if (core == 0) == (stage == 0):
                        target = device_number(y, 3 - x if far else x ^ 1, z, core)
                    else:
                        target = device_number(3 - y if far else y ^ 1, x, z, core)
                    pairs.append((source, target))
    return lax.ppermute(value, AXES, pairs)


def z_swap(value, far):
    pairs = [(0, 3), (3, 0), (1, 2), (2, 1)] if far else [(0, 1), (1, 0), (2, 3), (3, 2)]
    return lax.ppermute(value, "z", pairs)


def core_send(value):
    return lax.ppermute(value, "core", [(0, 1), (1, 0)])


VMEM = pl.BlockSpec(memory_space=pltpu.VMEM)
HBM = pl.BlockSpec(memory_space=pltpu.HBM)


class Chain:
    def __init__(self):
        self.last = None

    def __call__(self, body, outs, *operands, in_specs=None, out_specs=None, scratch=(), limit=8, cost=0, last=False):
        specs = [VMEM] * len(operands) if in_specs is None else list(in_specs)
        count, made = len(operands), len(outs)
        if self.last is not None:
            operands = operands + (self.last,)
            specs.append(VMEM)
        operands = [
            pltpu.with_memory_space_constraint(operand, spec.memory_space)
            for operand, spec in zip(operands, specs)
        ]

        def kernel(*refs):
            given, rest = refs[:count], refs[len(operands) :]
            if not last:
                token, rest = rest[made], rest[:made] + rest[made + 1 :]
                token[...] = jnp.zeros_like(token)
            body(*given, *rest)

        token_out, token_spec = ([], []) if last else ([pltpu.VMEM((8, 128), F32)], [VMEM])
        result = pl.pallas_call(
            kernel,
            name=body.__name__,
            out_shape=[*outs, *token_out],
            in_specs=specs,
            out_specs=[*([VMEM] * made if out_specs is None else out_specs), *token_spec],
            scratch_shapes=scratch,
            compiler_params=pltpu.CompilerParams(vmem_limit_bytes=limit * 2**20),
            cost_estimate=pl.CostEstimate(flops=cost, bytes_accessed=0, transcendentals=0),
        )(*operands)
        if not last:
            *result, self.last = result
        return result


def wide(*terms):
    total = terms[0].astype(F32)
    for term in terms[1:]:
        total = total + term.astype(F32)
    return total


def picked(rows, projection, contract):
    place = lax.broadcasted_iota(jnp.int32, (256, 256), 1)
    chosen = jnp.where(rows == place, 1.0, 0.0).astype(BF16)
    return lax.dot_general(chosen, projection, (((1,), (contract,)), ((), ())), preferred_element_type=F32).astype(BF16)


def fsdp_rows():
    y, x, core = lax.axis_index("y"), lax.axis_index("x"), lax.axis_index("core")
    step = lax.broadcasted_iota(jnp.int32, (256, 1), 0)
    outer, inner = step // 64, step // 16 % 4
    outer = jnp.where(outer == 0, 2, jnp.where(outer == 3, 0, jnp.where(outer == 1, 1, 3)))
    inner = jnp.where(inner == 1, 2, jnp.where(inner == 2, 1, inner))
    on_x, on_y = jnp.where(core == 0, outer, inner), jnp.where(core == 0, inner, outer)
    return ((y + on_y) % 4 * 4 + (x + on_x) % 4) * 16 + step % 16


def row_rows():
    z, core = lax.axis_index("z"), lax.axis_index("core")
    step = lax.broadcasted_iota(jnp.int32, (256, 1), 0)
    turn = step // 32 % 4
    to = jnp.where(turn % 2 == 0, z, 3 - z)
    to = jnp.where(turn < 2, to, to + 1 - to % 2 * 2)
    return (to * 2 + (core + step // 128) % 2) * 32 + step % 32


PARTS = tuple(range(0, 3200, 640))


def first_kernel(gate_proj, gate, up_proj, up, forth, back, gate_rest, up_rest, gate_kept, up_kept, projs, sems):
    proj_copies = [
        pltpu.make_async_copy(source, projs.at[index], sems.at[index]) for index, source in enumerate((gate_proj, up_proj))
    ]
    parts = ((0, 0, 1664), (0, 1664, 1536), (1, 0, 1664), (1, 1664, 1536))
    copies = []
    for number, (index, at, size) in enumerate(parts):
        source, target = ((gate, gate_kept), (up, up_kept))[index]
        to = pl.ds(at, size)
        copies.append(pltpu.make_async_copy(source.at[:, to], target.at[:, to], sems.at[2 + number]))
    for copy in proj_copies + copies:
        copy.start()
    rows = fsdp_rows()
    ordered = []
    for index, rest in enumerate((gate_rest, up_rest)):
        proj_copies[index].wait()
        ordered.append(picked(rows, projs[index], 1))
        rest[...] = ordered[index][64:]
    for copy, (index, start, size) in zip(copies, parts):
        copy.wait()
        kept = (gate_kept, up_kept)[index]
        for at in range(start, start + size, 512):
            width = min(512, start + size - at)
            part = jnp.dot(ordered[index][:64], kept[:, at : at + width], preferred_element_type=F32).astype(BF16)
            base = index * 3200 + at
            forth[:, base : base + width] = part[:32]
            back[:, base : base + width] = part[32:]


def rest_kernel(gate_rest, gate, up_rest, up, forth, back, near, far, keep):
    for rest, grad, base in ((gate_rest, gate, 0), (up_rest, up, 3200)):
        for at in range(0, 3200, 640):
            to = slice(base + at, base + at + 640)
            part = jnp.dot(rest[...], grad[:, at : at + 640], preferred_element_type=F32).astype(BF16)
            near[:, to] = part[:32]
            forth[:, to] = part[32:64]
            back[:, to] = part[64:96]
            far[:, to] = part[96:128]
            keep[:, to] = part[128:]


def pass_kernel(near, from_below, far, from_above, onward, backward):
    onward[...] = wide(near[...], from_below[...]).astype(BF16)
    backward[...] = wide(far[...], from_above[...]).astype(BF16)


def collect_kernel(keep, high_below, low_above, low, high):
    low[...] = wide(keep[:32], low_above[...])
    high[...] = wide(keep[32:], high_below[...])


def near_kernel(low, low_below, own, opposite):
    total = wide(low[...], low_below[...])
    own[...] = total[:16]
    opposite[...] = total[16:].astype(BF16)


def far_kernel(high, high_above, above, below):
    total = wide(high[...], high_above[...]).astype(BF16)
    above[...] = total[:16]
    below[...] = total[16:]


def moments(projected, first, second):
    return (
        beta_first * first[...] + (1.0 - beta_first) * projected,
        beta_second * second[...] + (1.0 - beta_second) * projected * projected,
    )


def channel_sums(projected, first, second):
    first_value, second_value = moments(projected, first, second)
    corrected = (first_value * (1.0 / (1.0 - beta_first**STEP))) / (
        jnp.sqrt(second_value * (1.0 / (1.0 - beta_second**STEP))) + adam_epsilon
    )
    return jnp.sum(corrected * corrected, 0, keepdims=True), jnp.sum(projected * projected, 0, keepdims=True)


def pair_sum_kernel(own, a, b, first_gate, second_gate, first_up, second_up, sums, sent, total):
    projected = wide(own[...], a[...], b[...])
    total[...] = projected
    sums[0:1], sums[1:2] = channel_sums(projected[:, :3200], first_gate, second_gate)
    sums[2:3], sums[3:4] = channel_sums(projected[:, 3200:], first_up, second_up)
    sent[...] = sums[...].astype(BF16)


def moment_kernel(total, total_d, first_gate, second_gate, first_up, second_up, first_down, second_down, *news):
    news[0][...], news[1][...] = moments(total[:, :3200], first_gate, second_gate)
    news[2][...], news[3][...] = moments(total[:, 3200:], first_up, second_up)
    news[4][...], news[5][...] = moments(total_d[...], first_down, second_down)


def down_sum_kernel(own, other, first, second, sums, sent, total):
    projected = wide(own[...], other[:64])
    total[...] = projected[:32]
    near = channel_sums(projected[:32], first, second)
    far = channel_sums(projected[32:], other[64:96].astype(F32), other[96:].astype(F32))
    sums[...] = jnp.zeros_like(sums)
    sums[0:1], sums[1:2] = near[0] + far[0], near[1] + far[1]
    sent[...] = sums[...].astype(BF16)


def add_kernel(*refs):
    refs[-1][...] = wide(*(ref[...] for ref in refs[:-1]))


def sum_kernel(*refs):
    total = wide(*(ref[...] for ref in refs[:-2]))
    refs[-2][...] = total
    refs[-1][...] = total.astype(BF16)


def scale_of(corrected_sq, projected_sq):
    return update_scale * (jnp.sqrt(corrected_sq) / (jnp.sqrt(projected_sq) + norm_epsilon))


def update_kernel(gate, up, own, other, gate_out, up_out, gate_made, up_made, sems):
    sums = wide(own[...], other[...])
    copies = []
    for index, (grad, made, out) in enumerate(((gate, gate_made, gate_out), (up, up_made, up_out))):
        scale = scale_of(sums[2 * index : 2 * index + 1], sums[2 * index + 1 : 2 * index + 2])
        made[...] = (grad[...].astype(F32) * scale).astype(BF16)
        copies.append(pltpu.make_async_copy(made, out, sems.at[index]))
        copies[-1].start()
    for copy in copies:
        copy.wait()


def down_kernel(proj, grad, own, other):
    ordered = picked(row_rows(), proj[...], 0)
    for at, size in ((0, 512), (512, 512), (1024, 576)):
        part = lax.dot_general(
            ordered, grad[at : at + size], (((1,), (1,)), ((), ())), preferred_element_type=F32
        ).astype(BF16)
        own[:, at : at + size] = part[:128]
        other[:, at : at + size] = part[128:]


def down_split_kernel(own, other, keep, send):
    total = wide(own[...], other[...])
    keep[...] = total[:64]
    send[...] = total[64:].astype(BF16)


def down_halve_kernel(own, other, first, second, keep, send):
    total = wide(own[...], other[...])
    keep[...] = total
    send[:32] = total[32:].astype(BF16)
    send[32:64] = total[:32].astype(BF16)
    send[64:96] = first[...].astype(BF16)
    send[96:] = second[...].astype(BF16)


def down_update_kernel(grad, own, other, out, scale):
    sums = wide(own[...], other[...])
    scale[:, :1600] = scale_of(sums[0:1], sums[1:2])
    for at in range(0, 1600, 128):
        size = min(128, 1600 - at)
        column = jnp.broadcast_to(scale[:, at : at + 128], (128, 128)).T[:size]
        for lane in range(0, 640, 128):
            block = grad[at : at + size, lane : lane + 128].astype(F32) * column
            out[at : at + size, lane : lane + 128] = block.astype(BF16)


def per_device(
    grad_gate,
    grad_up,
    grad_down,
    proj_gate,
    proj_up,
    proj_down,
    first_gate,
    second_gate,
    first_up,
    second_up,
    first_down,
    second_down,
):
    gate, up, down = grad_gate.T, grad_up.T, grad_down.T
    run = Chain()
    half, piece = pltpu.VMEM((32, 6400), BF16), pltpu.VMEM((16, 6400), BF16)
    part, held = pltpu.VMEM((192, 320), BF16), pltpu.VMEM((320, 3200), BF16)
    row, pair_row = pltpu.VMEM((8, 1600), F32), pltpu.VMEM((4, 3200), F32)
    sent_row, sent_pair = pltpu.VMEM((8, 1600), BF16), pltpu.VMEM((4, 3200), BF16)
    whole = jax.ShapeDtypeStruct((320, 3200), BF16)
    state, down_state = jax.ShapeDtypeStruct((16, 3200), F32), jax.ShapeDtypeStruct((32, 1600), F32)

    forth, back, rest_g, rest_u, gate, up = run(
        first_kernel,
        (half, half, part, part, held, held),
        proj_gate.T, gate, proj_up.T, up,
        in_specs=(HBM,) * 4,
        scratch=(pltpu.VMEM((2, 320, 256), BF16), pltpu.SemaphoreType.DMA((6,))),
    )
    from_below, from_above = ring_send(forth, 1, 0), ring_send(back, 3, 0)
    forth, back, near, far, keep = run(
        rest_kernel, (half, half, half, half, pltpu.VMEM((64, 6400), BF16)), rest_g, gate, rest_u, up
    )
    high_below, low_above = ring_send(forth, 1, 0), ring_send(back, 3, 0)
    own_down, other_down = run(down_kernel, (pltpu.VMEM((128, 1600), BF16),) * 2, proj_down, down)
    other_down = core_send(other_down)
    forth, back = run(pass_kernel, (half, half), near, from_below, far, from_above)
    low_below, high_above = ring_send(forth, 1, 0), ring_send(back, 3, 0)
    low, high = run(collect_kernel, (pltpu.VMEM((32, 6400), F32),) * 2, keep, high_below, low_above)
    own_down, other_down = run(
        down_split_kernel, (pltpu.VMEM((64, 1600), F32), pltpu.VMEM((64, 1600), BF16)), own_down, other_down
    )
    other_down = z_swap(other_down, False)

    own, opposite = run(near_kernel, (pltpu.VMEM((16, 6400), F32), piece), low, low_below)
    opposite = ring_send(opposite, 2, 1)
    above, below = run(far_kernel, (piece, piece), high, high_above)
    above, below = ring_send(above, 1, 1), ring_send(below, 3, 1)
    own_down, other_down = run(
        down_halve_kernel,
        (pltpu.VMEM((64, 1600), F32), pltpu.VMEM((128, 1600), BF16)),
        own_down, other_down, first_down, second_down,
    )
    other_down = z_swap(other_down, True)

    states = (first_gate, second_gate, first_up, second_up)
    (own,) = run(add_kernel, (pltpu.VMEM((16, 6400), F32),), own, opposite)
    sums, sent, total = run(
        pair_sum_kernel, (pair_row, sent_pair, pltpu.VMEM((16, 6400), F32)), own, above, below, *states,
        cost=8 * 10**9,
    )
    other = ring_swap(sent, False, 1)
    sums, sent = run(sum_kernel, (pair_row, sent_pair), sums, other)
    other = ring_swap(sent, True, 1)
    sums_d, sent_d, total_d = run(
        down_sum_kernel, (row, sent_row, pltpu.VMEM((32, 1600), F32)), own_down, other_down, first_down, second_down
    )
    other_d = z_swap(sent_d, False)
    sums, sent = run(sum_kernel, (pair_row, sent_pair), sums, other)
    other = ring_swap(sent, False, 0)
    sums_d, sent_d = run(sum_kernel, (row, sent_row), sums_d, other_d)
    other_d = core_send(sent_d)
    news = run(moment_kernel, (state,) * 4 + (down_state,) * 2, total, total_d, *states, first_down, second_down)
    sums, sent = run(sum_kernel, (pair_row, sent_pair), sums, other)
    other = ring_swap(sent, True, 0)
    (update_down,) = run(
        down_update_kernel,
        (jax.ShapeDtypeStruct((1600, 640), BF16),),
        down, sums_d, other_d,
        scratch=(pltpu.VMEM((1, 1664), F32),),
    )
    update_gate, update_up = run(
        update_kernel,
        (whole, whole),
        gate, up, sums, other,
        out_specs=(HBM, HBM),
        scratch=(held, held, pltpu.SemaphoreType.DMA((2,))),
        last=True,
    )
    return (
        update_gate.T,
        update_up.T,
        update_down.T,
        *news,
    )


def solution(mesh):
    fine = Mesh(mesh.devices.reshape(SIZES), AXES)
    gradient, state = P(ACROSS, ALONG), P(ALONG, ACROSS)
    return jax.shard_map(
        per_device,
        mesh=fine,
        in_specs=(
            gradient,
            gradient,
            gradient,
            P(None, ALONG),
            P(None, ALONG),
            P(None, ACROSS),
            state,
            state,
            state,
            state,
            gradient,
            gradient,
        ),
        out_specs=(
            gradient,
            gradient,
            gradient,
            state,
            state,
            state,
            state,
            gradient,
            gradient,
        ),
        check_vma=False,
    )
```

```python
import jax
import jax.numpy as jnp
from jax import lax
from jax.experimental import pallas as pl
from jax.experimental.pallas import tpu as pltpu
from jax.sharding import Mesh
from jax.sharding import PartitionSpec as P

STEP = 100

beta_first = 0.9
beta_second = 0.999
adam_epsilon = 1e-08
norm_epsilon = 1e-06
update_scale = 4.0

AXES = ("y", "x", "z", "core")
SIZES = (4, 4, 4, 2)
ALONG = ("y", "x")
ACROSS = ("z", "core")
F32 = jnp.float32
BF16 = jnp.bfloat16


def device_number(y, x, z, core):
    return ((y * 4 + x) * 4 + z) * 2 + core


def ring_pairs(shift, stage):
    pairs = []
    for y in range(4):
        for x in range(4):
            for z in range(4):
                for core in range(2):
                    source = device_number(y, x, z, core)
                    if (core == 0) == (stage == 0):
                        target = device_number(y, (x + shift) % 4, z, core)
                    else:
                        target = device_number((y + shift) % 4, x, z, core)
                    pairs.append((source, target))
    return pairs


def ring_send(value, shift, stage):
    return lax.ppermute(value, AXES, ring_pairs(shift, stage))


def ring_swap(value, far, stage):
    pairs = []
    for y in range(4):
        for x in range(4):
            for z in range(4):
                for core in range(2):
                    source = device_number(y, x, z, core)
                    if (core == 0) == (stage == 0):
                        target = device_number(y, 3 - x if far else x ^ 1, z, core)
                    else:
                        target = device_number(3 - y if far else y ^ 1, x, z, core)
                    pairs.append((source, target))
    return lax.ppermute(value, AXES, pairs)


def z_swap(value, far):
    pairs = [(0, 3), (3, 0), (1, 2), (2, 1)] if far else [(0, 1), (1, 0), (2, 3), (3, 2)]
    return lax.ppermute(value, "z", pairs)


def core_send(value):
    return lax.ppermute(value, "core", [(0, 1), (1, 0)])


VMEM = pl.BlockSpec(memory_space=pltpu.VMEM)
HBM = pl.BlockSpec(memory_space=pltpu.HBM)


class Chain:
    def __init__(self):
        self.last = None

    def __call__(self, body, outs, *operands, in_specs=None, out_specs=None, scratch=(), limit=8, cost=0, last=False):
        specs = [VMEM] * len(operands) if in_specs is None else list(in_specs)
        count, made = len(operands), len(outs)
        if self.last is not None:
            operands = operands + (self.last,)
            specs.append(VMEM)
        operands = [
            pltpu.with_memory_space_constraint(operand, spec.memory_space)
            for operand, spec in zip(operands, specs)
        ]

        def kernel(*refs):
            given, rest = refs[:count], refs[len(operands) :]
            if not last:
                token, rest = rest[made], rest[:made] + rest[made + 1 :]
                token[...] = jnp.zeros_like(token)
            body(*given, *rest)

        token_out, token_spec = ([], []) if last else ([pltpu.VMEM((8, 128), F32)], [VMEM])
        result = pl.pallas_call(
            kernel,
            name=body.__name__,
            out_shape=[*outs, *token_out],
            in_specs=specs,
            out_specs=[*([VMEM] * made if out_specs is None else out_specs), *token_spec],
            scratch_shapes=scratch,
            compiler_params=pltpu.CompilerParams(vmem_limit_bytes=limit * 2**20),
            cost_estimate=pl.CostEstimate(flops=cost, bytes_accessed=0, transcendentals=0),
        )(*operands)
        if not last:
            *result, self.last = result
        return result


def wide(*terms):
    total = terms[0].astype(F32)
    for term in terms[1:]:
        total = total + term.astype(F32)
    return total


def picked(rows, projection, contract):
    place = lax.broadcasted_iota(jnp.int32, (256, 256), 1)
    chosen = jnp.where(rows == place, 1.0, 0.0).astype(BF16)
    return lax.dot_general(chosen, projection, (((1,), (contract,)), ((), ())), preferred_element_type=F32).astype(BF16)


def fsdp_rows():
    y, x, core = lax.axis_index("y"), lax.axis_index("x"), lax.axis_index("core")
    step = lax.broadcasted_iota(jnp.int32, (256, 1), 0)
    outer, inner = step // 64, step // 16 % 4
    outer = jnp.where(outer == 0, 2, jnp.where(outer == 3, 0, jnp.where(outer == 1, 1, 3)))
    on_x, on_y = jnp.where(core == 0, outer, inner), jnp.where(core == 0, inner, outer)
    return ((y + on_y) % 4 * 4 + (x + on_x) % 4) * 16 + step % 16


def row_rows():
    z, core = lax.axis_index("z"), lax.axis_index("core")
    step = lax.broadcasted_iota(jnp.int32, (256, 1), 0)
    turn = step // 32 % 4
    to = jnp.where(turn % 2 == 0, z, 3 - z)
    to = jnp.where(turn < 2, to, to + 1 - to % 2 * 2)
    return (to * 2 + (core + step // 128) % 2) * 32 + step % 32


PARTS = tuple(range(0, 3200, 640))


def first_kernel(gate_proj, gate, up_proj, up, forth, back, gate_rest, up_rest, gate_kept, up_kept, projs, sems):
    proj_copies = [
        pltpu.make_async_copy(source, projs.at[index], sems.at[index]) for index, source in enumerate((gate_proj, up_proj))
    ]
    parts = ((0, 0, 1664), (0, 1664, 1536), (1, 0, 1664), (1, 1664, 1536))
    copies = []
    for number, (index, at, size) in enumerate(parts):
        source, target = ((gate, gate_kept), (up, up_kept))[index]
        to = pl.ds(at, size)
        copies.append(pltpu.make_async_copy(source.at[:, to], target.at[:, to], sems.at[2 + number]))
    for copy in proj_copies + copies:
        copy.start()
    rows = fsdp_rows()
    ordered = []
    for index, rest in enumerate((gate_rest, up_rest)):
        proj_copies[index].wait()
        ordered.append(picked(rows, projs[index], 1))
        rest[...] = ordered[index][64:]
    for copy, (index, start, size) in zip(copies, parts):
        copy.wait()
        kept = (gate_kept, up_kept)[index]
        for at in range(start, start + size, 512):
            width = min(512, start + size - at)
            part = jnp.dot(ordered[index][:64], kept[:, at : at + width], preferred_element_type=F32).astype(BF16)
            base = index * 3200 + at
            forth[:, base : base + width] = part[:32]
            back[:, base : base + width] = part[32:]


def rest_kernel(gate_rest, gate, up_rest, up, forth, back, near, far, keep):
    for rest, grad, base in ((gate_rest, gate, 0), (up_rest, up, 3200)):
        for at in range(0, 3200, 640):
            to = slice(base + at, base + at + 640)
            part = jnp.dot(rest[...], grad[:, at : at + 640], preferred_element_type=F32).astype(BF16)
            near[:, to] = part[:32]
            forth[:, to] = part[32:64]
            back[:, to] = part[64:96]
            far[:, to] = part[96:128]
            keep[:, to] = part[128:]


def pass_kernel(near, from_below, far, from_above, onward, backward):
    onward[...] = wide(near[...], from_below[...]).astype(BF16)
    backward[...] = wide(far[...], from_above[...]).astype(BF16)


def collect_kernel(keep, high_below, low_above, low, high):
    low[...] = wide(keep[:32], low_above[...])
    high[...] = wide(keep[32:], high_below[...])


def near_kernel(low, low_below, own, above):
    total = wide(low[...], low_below[...])
    own[...] = total[:16]
    above[...] = total[16:].astype(BF16)


def far_kernel(high, high_above, opposite, below):
    total = wide(high[...], high_above[...]).astype(BF16)
    opposite[...] = total[:16]
    below[...] = total[16:]


def moments(projected, first, second):
    return (
        beta_first * first[...] + (1.0 - beta_first) * projected,
        beta_second * second[...] + (1.0 - beta_second) * projected * projected,
    )


def channel_sums(projected, first, second):
    first_value, second_value = moments(projected, first, second)
    corrected = (first_value * (1.0 / (1.0 - beta_first**STEP))) / (
        jnp.sqrt(second_value * (1.0 / (1.0 - beta_second**STEP))) + adam_epsilon
    )
    return jnp.sum(corrected * corrected, 0, keepdims=True), jnp.sum(projected * projected, 0, keepdims=True)


def pair_sum_kernel(own, a, b, first_gate, second_gate, first_up, second_up, sums, sent, total):
    projected = wide(own[...], a[...], b[...])
    total[...] = projected
    sums[0:1], sums[1:2] = channel_sums(projected[:, :3200], first_gate, second_gate)
    sums[2:3], sums[3:4] = channel_sums(projected[:, 3200:], first_up, second_up)
    sent[...] = sums[...].astype(BF16)


def moment_kernel(total, total_d, first_gate, second_gate, first_up, second_up, first_down, second_down, *news):
    news[0][...], news[1][...] = moments(total[:, :3200], first_gate, second_gate)
    news[2][...], news[3][...] = moments(total[:, 3200:], first_up, second_up)
    news[4][...], news[5][...] = moments(total_d[...], first_down, second_down)


def down_sum_kernel(own, other, first, second, sums, sent, total):
    projected = wide(own[...], other[:64])
    total[...] = projected[:32]
    near = channel_sums(projected[:32], first, second)
    far = channel_sums(projected[32:], other[64:96].astype(F32), other[96:].astype(F32))
    sums[...] = jnp.zeros_like(sums)
    sums[0:1], sums[1:2] = near[0] + far[0], near[1] + far[1]
    sent[...] = sums[...].astype(BF16)


def add_kernel(*refs):
    refs[-1][...] = wide(*(ref[...] for ref in refs[:-1]))


def sum_kernel(*refs):
    total = wide(*(ref[...] for ref in refs[:-2]))
    refs[-2][...] = total
    refs[-1][...] = total.astype(BF16)


def scale_of(corrected_sq, projected_sq):
    return update_scale * (jnp.sqrt(corrected_sq) / (jnp.sqrt(projected_sq) + norm_epsilon))


def update_kernel(gate, up, own, other, gate_out, up_out, gate_made, up_made, sems):
    sums = wide(own[...], other[...])
    copies = []
    for index, (grad, made, out) in enumerate(((gate, gate_made, gate_out), (up, up_made, up_out))):
        scale = scale_of(sums[2 * index : 2 * index + 1], sums[2 * index + 1 : 2 * index + 2])
        made[...] = (grad[...].astype(F32) * scale).astype(BF16)
        copies.append(pltpu.make_async_copy(made, out, sems.at[index]))
        copies[-1].start()
    for copy in copies:
        copy.wait()


def down_kernel(proj, grad, own, other):
    ordered = picked(row_rows(), proj[...], 0)
    for at, size in ((0, 512), (512, 512), (1024, 576)):
        part = lax.dot_general(
            ordered, grad[at : at + size], (((1,), (1,)), ((), ())), preferred_element_type=F32
        ).astype(BF16)
        own[:, at : at + size] = part[:128]
        other[:, at : at + size] = part[128:]


def down_split_kernel(own, other, keep, send):
    total = wide(own[...], other[...])
    keep[...] = total[:64]
    send[...] = total[64:].astype(BF16)


def down_halve_kernel(own, other, first, second, keep, send):
    total = wide(own[...], other[...])
    keep[...] = total
    send[:32] = total[32:].astype(BF16)
    send[32:64] = total[:32].astype(BF16)
    send[64:96] = first[...].astype(BF16)
    send[96:] = second[...].astype(BF16)


def down_update_kernel(grad, own, other, out, scale):
    sums = wide(own[...], other[...])
    scale[:, :1600] = scale_of(sums[0:1], sums[1:2])
    for at in range(0, 1600, 128):
        size = min(128, 1600 - at)
        column = jnp.broadcast_to(scale[:, at : at + 128], (128, 128)).T[:size]
        for lane in range(0, 640, 128):
            block = grad[at : at + size, lane : lane + 128].astype(F32) * column
            out[at : at + size, lane : lane + 128] = block.astype(BF16)


def per_device(
    grad_gate,
    grad_up,
    grad_down,
    proj_gate,
    proj_up,
    proj_down,
    first_gate,
    second_gate,
    first_up,
    second_up,
    first_down,
    second_down,
):
    gate, up, down = grad_gate.T, grad_up.T, grad_down.T
    run = Chain()
    half, piece = pltpu.VMEM((32, 6400), BF16), pltpu.VMEM((16, 6400), BF16)
    part, held = pltpu.VMEM((192, 320), BF16), pltpu.VMEM((320, 3200), BF16)
    row, pair_row = pltpu.VMEM((8, 1600), F32), pltpu.VMEM((4, 3200), F32)
    sent_row, sent_pair = pltpu.VMEM((8, 1600), BF16), pltpu.VMEM((4, 3200), BF16)
    whole = jax.ShapeDtypeStruct((320, 3200), BF16)
    state, down_state = jax.ShapeDtypeStruct((16, 3200), F32), jax.ShapeDtypeStruct((32, 1600), F32)

    forth, back, rest_g, rest_u, gate, up = run(
        first_kernel,
        (half, half, part, part, held, held),
        proj_gate.T, gate, proj_up.T, up,
        in_specs=(HBM,) * 4,
        scratch=(pltpu.VMEM((2, 320, 256), BF16), pltpu.SemaphoreType.DMA((6,))),
    )
    from_below, from_above = ring_send(forth, 1, 0), ring_send(back, 3, 0)
    forth, back, near, far, keep = run(
        rest_kernel, (half, half, half, half, pltpu.VMEM((64, 6400), BF16)), rest_g, gate, rest_u, up
    )
    high_below, low_above = ring_send(forth, 1, 0), ring_send(back, 3, 0)
    own_down, other_down = run(down_kernel, (pltpu.VMEM((128, 1600), BF16),) * 2, proj_down, down)
    other_down = core_send(other_down)
    forth, back = run(pass_kernel, (half, half), near, from_below, far, from_above)
    low_below, high_above = ring_send(forth, 1, 0), ring_send(back, 3, 0)
    low, high = run(collect_kernel, (pltpu.VMEM((32, 6400), F32),) * 2, keep, high_below, low_above)
    own_down, other_down = run(
        down_split_kernel, (pltpu.VMEM((64, 1600), F32), pltpu.VMEM((64, 1600), BF16)), own_down, other_down
    )
    other_down = z_swap(other_down, False)

    own, above = run(near_kernel, (pltpu.VMEM((16, 6400), F32), piece), low, low_below)
    above = ring_send(above, 1, 1)
    opposite, below = run(far_kernel, (piece, piece), high, high_above)
    opposite, below = ring_send(opposite, 2, 1), ring_send(below, 3, 1)
    own_down, other_down = run(
        down_halve_kernel,
        (pltpu.VMEM((64, 1600), F32), pltpu.VMEM((128, 1600), BF16)),
        own_down, other_down, first_down, second_down,
    )
    other_down = z_swap(other_down, True)

    states = (first_gate, second_gate, first_up, second_up)
    (own,) = run(add_kernel, (pltpu.VMEM((16, 6400), F32),), own, above)
    sums, sent, total = run(
        pair_sum_kernel, (pair_row, sent_pair, pltpu.VMEM((16, 6400), F32)), own, below, opposite, *states,
        cost=8 * 10**9,
    )
    other = ring_swap(sent, False, 1)
    sums, sent = run(sum_kernel, (pair_row, sent_pair), sums, other)
    other = ring_swap(sent, True, 1)
    sums_d, sent_d, total_d = run(
        down_sum_kernel, (row, sent_row, pltpu.VMEM((32, 1600), F32)), own_down, other_down, first_down, second_down
    )
    other_d = z_swap(sent_d, False)
    sums, sent = run(sum_kernel, (pair_row, sent_pair), sums, other)
    other = ring_swap(sent, False, 0)
    sums_d, sent_d = run(sum_kernel, (row, sent_row), sums_d, other_d)
    other_d = core_send(sent_d)
    news = run(moment_kernel, (state,) * 4 + (down_state,) * 2, total, total_d, *states, first_down, second_down)
    sums, sent = run(sum_kernel, (pair_row, sent_pair), sums, other)
    other = ring_swap(sent, True, 0)
    (update_down,) = run(
        down_update_kernel,
        (jax.ShapeDtypeStruct((1600, 640), BF16),),
        down, sums_d, other_d,
        scratch=(pltpu.VMEM((1, 1664), F32),),
    )
    update_gate, update_up = run(
        update_kernel,
        (whole, whole),
        gate, up, sums, other,
        out_specs=(HBM, HBM),
        scratch=(held, held, pltpu.SemaphoreType.DMA((2,))),
        last=True,
    )
    return (
        update_gate.T,
        update_up.T,
        update_down.T,
        *news,
    )


def solution(mesh):
    fine = Mesh(mesh.devices.reshape(SIZES), AXES)
    gradient, state = P(ACROSS, ALONG), P(ALONG, ACROSS)
    return jax.shard_map(
        per_device,
        mesh=fine,
        in_specs=(
            gradient,
            gradient,
            gradient,
            P(None, ALONG),
            P(None, ALONG),
            P(None, ACROSS),
            state,
            state,
            state,
            state,
            gradient,
            gradient,
        ),
        out_specs=(
            gradient,
            gradient,
            gradient,
            state,
            state,
            state,
            state,
            gradient,
            gradient,
        ),
        check_vma=False,
    )
```

```python
import jax
import jax.numpy as jnp
from jax import lax
from jax.experimental import pallas as pl
from jax.experimental.pallas import tpu as pltpu
from jax.sharding import Mesh
from jax.sharding import PartitionSpec as P

STEP = 100

beta_first = 0.9
beta_second = 0.999
adam_epsilon = 1e-08
norm_epsilon = 1e-06
update_scale = 4.0

AXES = ("y", "x", "z", "core")
SIZES = (4, 4, 4, 2)
ALONG = ("y", "x")
ACROSS = ("z", "core")
F32 = jnp.float32
BF16 = jnp.bfloat16


def device_number(y, x, z, core):
    return ((y * 4 + x) * 4 + z) * 2 + core


def ring_pairs(shift, stage):
    pairs = []
    for y in range(4):
        for x in range(4):
            for z in range(4):
                for core in range(2):
                    source = device_number(y, x, z, core)
                    if (core == 0) == (stage == 0):
                        target = device_number(y, (x + shift) % 4, z, core)
                    else:
                        target = device_number((y + shift) % 4, x, z, core)
                    pairs.append((source, target))
    return pairs


def ring_send(value, shift, stage):
    return lax.ppermute(value, AXES, ring_pairs(shift, stage))


def ring_swap(value, far, stage):
    pairs = []
    for y in range(4):
        for x in range(4):
            for z in range(4):
                for core in range(2):
                    source = device_number(y, x, z, core)
                    if (core == 0) == (stage == 0):
                        target = device_number(y, 3 - x if far else x ^ 1, z, core)
                    else:
                        target = device_number(3 - y if far else y ^ 1, x, z, core)
                    pairs.append((source, target))
    return lax.ppermute(value, AXES, pairs)


def z_swap(value, far):
    pairs = [(0, 3), (3, 0), (1, 2), (2, 1)] if far else [(0, 1), (1, 0), (2, 3), (3, 2)]
    return lax.ppermute(value, "z", pairs)


def core_send(value):
    return lax.ppermute(value, "core", [(0, 1), (1, 0)])


VMEM = pl.BlockSpec(memory_space=pltpu.VMEM)
HBM = pl.BlockSpec(memory_space=pltpu.HBM)


class Chain:
    def __init__(self):
        self.last = None

    def __call__(self, body, outs, *operands, in_specs=None, out_specs=None, scratch=(), limit=8, cost=0, last=False):
        specs = [VMEM] * len(operands) if in_specs is None else list(in_specs)
        count, made = len(operands), len(outs)
        if self.last is not None:
            operands = operands + (self.last,)
            specs.append(VMEM)
        operands = [
            pltpu.with_memory_space_constraint(operand, spec.memory_space)
            for operand, spec in zip(operands, specs)
        ]

        def kernel(*refs):
            given, rest = refs[:count], refs[len(operands) :]
            if not last:
                token, rest = rest[made], rest[:made] + rest[made + 1 :]
                token[...] = jnp.zeros_like(token)
            body(*given, *rest)

        token_out, token_spec = ([], []) if last else ([pltpu.VMEM((8, 128), F32)], [VMEM])
        result = pl.pallas_call(
            kernel,
            name=body.__name__,
            out_shape=[*outs, *token_out],
            in_specs=specs,
            out_specs=[*([VMEM] * made if out_specs is None else out_specs), *token_spec],
            scratch_shapes=scratch,
            compiler_params=pltpu.CompilerParams(vmem_limit_bytes=limit * 2**20),
            cost_estimate=pl.CostEstimate(flops=cost, bytes_accessed=0, transcendentals=0),
        )(*operands)
        if not last:
            *result, self.last = result
        return result


def wide(*terms):
    total = terms[0].astype(F32)
    for term in terms[1:]:
        total = total + term.astype(F32)
    return total


def picked(rows, projection, contract):
    place = lax.broadcasted_iota(jnp.int32, (256, 256), 1)
    chosen = jnp.where(rows == place, 1.0, 0.0).astype(BF16)
    return lax.dot_general(chosen, projection, (((1,), (contract,)), ((), ())), preferred_element_type=F32).astype(BF16)


def fsdp_rows():
    y, x, core = lax.axis_index("y"), lax.axis_index("x"), lax.axis_index("core")
    step = lax.broadcasted_iota(jnp.int32, (256, 1), 0)
    outer, inner = step // 64, step // 16 % 4
    outer = jnp.where(outer == 0, 2, jnp.where(outer == 3, 0, jnp.where(outer == 1, 1, 3)))
    on_x, on_y = jnp.where(core == 0, outer, inner), jnp.where(core == 0, inner, outer)
    return ((y + on_y) % 4 * 4 + (x + on_x) % 4) * 16 + step % 16


def row_rows():
    z, core = lax.axis_index("z"), lax.axis_index("core")
    step = lax.broadcasted_iota(jnp.int32, (256, 1), 0)
    turn = step // 32 % 4
    to = jnp.where(turn % 2 == 0, z, 3 - z)
    to = jnp.where(turn < 2, to, to + 1 - to % 2 * 2)
    return (to * 2 + (core + step // 128) % 2) * 32 + step % 32


PARTS = tuple(range(0, 3200, 640))


def first_kernel(gate_proj, gate, up_proj, up, forth, back, gate_rest, up_rest, gate_kept, up_kept, projs, sems):
    proj_copies = [
        pltpu.make_async_copy(source, projs.at[index], sems.at[index]) for index, source in enumerate((gate_proj, up_proj))
    ]
    parts = ((0, 0, 1664), (0, 1664, 1536), (1, 0, 1664), (1, 1664, 1536))
    copies = []
    for number, (index, at, size) in enumerate(parts):
        source, target = ((gate, gate_kept), (up, up_kept))[index]
        to = pl.ds(at, size)
        copies.append(pltpu.make_async_copy(source.at[:, to], target.at[:, to], sems.at[2 + number]))
    for copy in proj_copies + copies:
        copy.start()
    rows = fsdp_rows()
    ordered = []
    for index, rest in enumerate((gate_rest, up_rest)):
        proj_copies[index].wait()
        ordered.append(picked(rows, projs[index], 1))
        rest[...] = ordered[index][64:]
    for copy, (index, start, size) in zip(copies, parts):
        copy.wait()
        kept = (gate_kept, up_kept)[index]
        for at in range(start, start + size, 512):
            width = min(512, start + size - at)
            part = jnp.dot(ordered[index][:64], kept[:, at : at + width], preferred_element_type=F32).astype(BF16)
            base = index * 3200 + at
            forth[:, base : base + width] = part[:32]
            back[:, base : base + width] = part[32:]


def rest_kernel(gate_rest, gate, up_rest, up, forth, back, near, far, keep):
    for rest, grad, base in ((gate_rest, gate, 0), (up_rest, up, 3200)):
        for at in range(0, 3200, 640):
            to = slice(base + at, base + at + 640)
            part = jnp.dot(rest[...], grad[:, at : at + 640], preferred_element_type=F32).astype(BF16)
            near[:, to] = part[:32]
            forth[:, to] = part[32:64]
            back[:, to] = part[64:96]
            far[:, to] = part[96:128]
            keep[:, to] = part[128:]


def pass_kernel(own, arrived, onward):
    onward[...] = wide(own[...], arrived[...]).astype(BF16)


def collect_kernel(keep, high_below, low_above, low, high):
    low[...] = wide(keep[:32], low_above[...])
    high[...] = wide(keep[32:], high_below[...])


def near_kernel(low, low_below, own, above):
    total = wide(low[...], low_below[...])
    own[...] = total[:16]
    above[...] = total[16:].astype(BF16)


def far_kernel(high, high_above, opposite, below):
    total = wide(high[...], high_above[...]).astype(BF16)
    opposite[...] = total[:16]
    below[...] = total[16:]


def moments(projected, first, second):
    return (
        beta_first * first[...] + (1.0 - beta_first) * projected,
        beta_second * second[...] + (1.0 - beta_second) * projected * projected,
    )


def channel_sums(projected, first, second):
    first_value, second_value = moments(projected, first, second)
    corrected = (first_value * (1.0 / (1.0 - beta_first**STEP))) / (
        jnp.sqrt(second_value * (1.0 / (1.0 - beta_second**STEP))) + adam_epsilon
    )
    return jnp.sum(corrected * corrected, 0, keepdims=True), jnp.sum(projected * projected, 0, keepdims=True)


def pair_sum_kernel(own, a, b, first_gate, second_gate, first_up, second_up, sums, sent, total):
    projected = wide(own[...], a[...], b[...])
    total[...] = projected
    sums[0:1], sums[1:2] = channel_sums(projected[:, :3200], first_gate, second_gate)
    sums[2:3], sums[3:4] = channel_sums(projected[:, 3200:], first_up, second_up)
    sent[...] = sums[...].astype(BF16)


def moment_kernel(total, total_d, first_gate, second_gate, first_up, second_up, first_down, second_down, *news):
    news[0][...], news[1][...] = moments(total[:, :3200], first_gate, second_gate)
    news[2][...], news[3][...] = moments(total[:, 3200:], first_up, second_up)
    news[4][...], news[5][...] = moments(total_d[...], first_down, second_down)


def down_sum_kernel(own, other, first, second, sums, sent, total):
    projected = wide(own[...], other[:64])
    total[...] = projected[:32]
    near = channel_sums(projected[:32], first, second)
    far = channel_sums(projected[32:], other[64:96].astype(F32), other[96:].astype(F32))
    sums[...] = jnp.zeros_like(sums)
    sums[0:1], sums[1:2] = near[0] + far[0], near[1] + far[1]
    sent[...] = sums[...].astype(BF16)


def add_kernel(*refs):
    refs[-1][...] = wide(*(ref[...] for ref in refs[:-1]))


def sum_kernel(*refs):
    total = wide(*(ref[...] for ref in refs[:-2]))
    refs[-2][...] = total
    refs[-1][...] = total.astype(BF16)


def scale_of(corrected_sq, projected_sq):
    return update_scale * (jnp.sqrt(corrected_sq) / (jnp.sqrt(projected_sq) + norm_epsilon))


def update_kernel(gate, up, own, other, gate_out, up_out, gate_made, up_made, sems):
    sums = wide(own[...], other[...])
    copies = []
    for index, (grad, made, out) in enumerate(((gate, gate_made, gate_out), (up, up_made, up_out))):
        scale = scale_of(sums[2 * index : 2 * index + 1], sums[2 * index + 1 : 2 * index + 2])
        made[...] = (grad[...].astype(F32) * scale).astype(BF16)
        copies.append(pltpu.make_async_copy(made, out, sems.at[index]))
        copies[-1].start()
    for copy in copies:
        copy.wait()


def down_kernel(proj, grad, own, other):
    ordered = picked(row_rows(), proj[...], 0)
    for at, size in ((0, 512), (512, 512), (1024, 576)):
        part = lax.dot_general(
            ordered, grad[at : at + size], (((1,), (1,)), ((), ())), preferred_element_type=F32
        ).astype(BF16)
        own[:, at : at + size] = part[:128]
        other[:, at : at + size] = part[128:]


def down_split_kernel(own, other, keep, send):
    total = wide(own[...], other[...])
    keep[...] = total[:64]
    send[...] = total[64:].astype(BF16)


def down_halve_kernel(own, other, first, second, keep, send):
    total = wide(own[...], other[...])
    keep[...] = total
    send[:32] = total[32:].astype(BF16)
    send[32:64] = total[:32].astype(BF16)
    send[64:96] = first[...].astype(BF16)
    send[96:] = second[...].astype(BF16)


def down_update_kernel(grad, own, other, out, scale):
    sums = wide(own[...], other[...])
    scale[:, :1600] = scale_of(sums[0:1], sums[1:2])
    for at in range(0, 1600, 128):
        size = min(128, 1600 - at)
        column = jnp.broadcast_to(scale[:, at : at + 128], (128, 128)).T[:size]
        for lane in range(0, 640, 128):
            block = grad[at : at + size, lane : lane + 128].astype(F32) * column
            out[at : at + size, lane : lane + 128] = block.astype(BF16)


def per_device(
    grad_gate,
    grad_up,
    grad_down,
    proj_gate,
    proj_up,
    proj_down,
    first_gate,
    second_gate,
    first_up,
    second_up,
    first_down,
    second_down,
):
    gate, up, down = grad_gate.T, grad_up.T, grad_down.T
    run = Chain()
    half, piece = pltpu.VMEM((32, 6400), BF16), pltpu.VMEM((16, 6400), BF16)
    part, held = pltpu.VMEM((192, 320), BF16), pltpu.VMEM((320, 3200), BF16)
    row, pair_row = pltpu.VMEM((8, 1600), F32), pltpu.VMEM((4, 3200), F32)
    sent_row, sent_pair = pltpu.VMEM((8, 1600), BF16), pltpu.VMEM((4, 3200), BF16)
    whole = jax.ShapeDtypeStruct((320, 3200), BF16)
    state, down_state = jax.ShapeDtypeStruct((16, 3200), F32), jax.ShapeDtypeStruct((32, 1600), F32)

    forth, back, rest_g, rest_u, gate, up = run(
        first_kernel,
        (half, half, part, part, held, held),
        proj_gate.T, gate, proj_up.T, up,
        in_specs=(HBM,) * 4,
        scratch=(pltpu.VMEM((2, 320, 256), BF16), pltpu.SemaphoreType.DMA((6,))),
    )
    from_below, from_above = ring_send(forth, 1, 0), ring_send(back, 3, 0)
    forth, back, near, far, keep = run(
        rest_kernel, (half, half, half, half, pltpu.VMEM((64, 6400), BF16)), rest_g, gate, rest_u, up
    )
    high_below, low_above = ring_send(forth, 1, 0), ring_send(back, 3, 0)
    own_down, other_down = run(down_kernel, (pltpu.VMEM((128, 1600), BF16),) * 2, proj_down, down)
    other_down = core_send(other_down)
    (forth,) = run(pass_kernel, (half,), near, from_below)
    low_below = ring_send(forth, 1, 0)
    (back,) = run(pass_kernel, (half,), far, from_above)
    high_above = ring_send(back, 3, 0)
    low, high = run(collect_kernel, (pltpu.VMEM((32, 6400), F32),) * 2, keep, high_below, low_above)
    own_down, other_down = run(
        down_split_kernel, (pltpu.VMEM((64, 1600), F32), pltpu.VMEM((64, 1600), BF16)), own_down, other_down
    )
    other_down = z_swap(other_down, False)

    own, above = run(near_kernel, (pltpu.VMEM((16, 6400), F32), piece), low, low_below)
    above = ring_send(above, 1, 1)
    opposite, below = run(far_kernel, (piece, piece), high, high_above)
    opposite, below = ring_send(opposite, 2, 1), ring_send(below, 3, 1)
    own_down, other_down = run(
        down_halve_kernel,
        (pltpu.VMEM((64, 1600), F32), pltpu.VMEM((128, 1600), BF16)),
        own_down, other_down, first_down, second_down,
    )
    other_down = z_swap(other_down, True)

    states = (first_gate, second_gate, first_up, second_up)
    (own,) = run(add_kernel, (pltpu.VMEM((16, 6400), F32),), own, above)
    sums, sent, total = run(
        pair_sum_kernel, (pair_row, sent_pair, pltpu.VMEM((16, 6400), F32)), own, below, opposite, *states,
        cost=8 * 10**9,
    )
    other = ring_swap(sent, False, 1)
    sums, sent = run(sum_kernel, (pair_row, sent_pair), sums, other)
    other = ring_swap(sent, True, 1)
    sums_d, sent_d, total_d = run(
        down_sum_kernel, (row, sent_row, pltpu.VMEM((32, 1600), F32)), own_down, other_down, first_down, second_down
    )
    other_d = z_swap(sent_d, False)
    sums, sent = run(sum_kernel, (pair_row, sent_pair), sums, other)
    other = ring_swap(sent, False, 0)
    sums_d, sent_d = run(sum_kernel, (row, sent_row), sums_d, other_d)
    other_d = core_send(sent_d)
    news = run(moment_kernel, (state,) * 4 + (down_state,) * 2, total, total_d, *states, first_down, second_down)
    sums, sent = run(sum_kernel, (pair_row, sent_pair), sums, other)
    other = ring_swap(sent, True, 0)
    (update_down,) = run(
        down_update_kernel,
        (jax.ShapeDtypeStruct((1600, 640), BF16),),
        down, sums_d, other_d,
        scratch=(pltpu.VMEM((1, 1664), F32),),
    )
    update_gate, update_up = run(
        update_kernel,
        (whole, whole),
        gate, up, sums, other,
        out_specs=(HBM, HBM),
        scratch=(held, held, pltpu.SemaphoreType.DMA((2,))),
        last=True,
    )
    return (
        update_gate.T,
        update_up.T,
        update_down.T,
        *news,
    )


def solution(mesh):
    fine = Mesh(mesh.devices.reshape(SIZES), AXES)
    gradient, state = P(ACROSS, ALONG), P(ALONG, ACROSS)
    return jax.shard_map(
        per_device,
        mesh=fine,
        in_specs=(
            gradient,
            gradient,
            gradient,
            P(None, ALONG),
            P(None, ALONG),
            P(None, ACROSS),
            state,
            state,
            state,
            state,
            gradient,
            gradient,
        ),
        out_specs=(
            gradient,
            gradient,
            gradient,
            state,
            state,
            state,
            state,
            gradient,
            gradient,
        ),
        check_vma=False,
    )
```

```python
import jax
import jax.numpy as jnp
from jax import lax
from jax.experimental import pallas as pl
from jax.experimental.pallas import tpu as pltpu
from jax.sharding import Mesh
from jax.sharding import PartitionSpec as P

STEP = 100

beta_first = 0.9
beta_second = 0.999
adam_epsilon = 1e-08
norm_epsilon = 1e-06
update_scale = 4.0

AXES = ("y", "x", "z", "core")
SIZES = (4, 4, 4, 2)
ALONG = ("y", "x")
ACROSS = ("z", "core")
F32 = jnp.float32
BF16 = jnp.bfloat16


def device_number(y, x, z, core):
    return ((y * 4 + x) * 4 + z) * 2 + core


def ring_pairs(shift, stage):
    pairs = []
    for y in range(4):
        for x in range(4):
            for z in range(4):
                for core in range(2):
                    source = device_number(y, x, z, core)
                    if (core == 0) == (stage == 0):
                        target = device_number(y, (x + shift) % 4, z, core)
                    else:
                        target = device_number((y + shift) % 4, x, z, core)
                    pairs.append((source, target))
    return pairs


def ring_send(value, shift, stage):
    return lax.ppermute(value, AXES, ring_pairs(shift, stage))


def ring_swap(value, far, stage):
    pairs = []
    for y in range(4):
        for x in range(4):
            for z in range(4):
                for core in range(2):
                    source = device_number(y, x, z, core)
                    if (core == 0) == (stage == 0):
                        target = device_number(y, 3 - x if far else x ^ 1, z, core)
                    else:
                        target = device_number(3 - y if far else y ^ 1, x, z, core)
                    pairs.append((source, target))
    return lax.ppermute(value, AXES, pairs)


def z_swap(value, far):
    pairs = [(0, 3), (3, 0), (1, 2), (2, 1)] if far else [(0, 1), (1, 0), (2, 3), (3, 2)]
    return lax.ppermute(value, "z", pairs)


def core_send(value):
    return lax.ppermute(value, "core", [(0, 1), (1, 0)])


VMEM = pl.BlockSpec(memory_space=pltpu.VMEM)
HBM = pl.BlockSpec(memory_space=pltpu.HBM)


class Chain:
    def __init__(self):
        self.last = None

    def __call__(self, body, outs, *operands, in_specs=None, out_specs=None, scratch=(), limit=8, cost=0, last=False):
        specs = [VMEM] * len(operands) if in_specs is None else list(in_specs)
        count, made = len(operands), len(outs)
        if self.last is not None:
            operands = operands + (self.last,)
            specs.append(VMEM)
        operands = [
            pltpu.with_memory_space_constraint(operand, spec.memory_space)
            for operand, spec in zip(operands, specs)
        ]

        def kernel(*refs):
            given, rest = refs[:count], refs[len(operands) :]
            if not last:
                token, rest = rest[made], rest[:made] + rest[made + 1 :]
                token[...] = jnp.zeros_like(token)
            body(*given, *rest)

        token_out, token_spec = ([], []) if last else ([pltpu.VMEM((8, 128), F32)], [VMEM])
        result = pl.pallas_call(
            kernel,
            name=body.__name__,
            out_shape=[*outs, *token_out],
            in_specs=specs,
            out_specs=[*([VMEM] * made if out_specs is None else out_specs), *token_spec],
            scratch_shapes=scratch,
            compiler_params=pltpu.CompilerParams(vmem_limit_bytes=limit * 2**20),
            cost_estimate=pl.CostEstimate(flops=cost, bytes_accessed=0, transcendentals=0),
        )(*operands)
        if not last:
            *result, self.last = result
        return result


def wide(*terms):
    total = terms[0].astype(F32)
    for term in terms[1:]:
        total = total + term.astype(F32)
    return total


def picked(rows, projection, contract):
    place = lax.broadcasted_iota(jnp.int32, (256, 256), 1)
    chosen = jnp.where(rows == place, 1.0, 0.0).astype(BF16)
    return lax.dot_general(chosen, projection, (((1,), (contract,)), ((), ())), preferred_element_type=F32).astype(BF16)


def fsdp_rows():
    y, x, core = lax.axis_index("y"), lax.axis_index("x"), lax.axis_index("core")
    step = lax.broadcasted_iota(jnp.int32, (256, 1), 0)
    outer, inner = step // 64, step // 16 % 4
    outer = jnp.where(outer == 0, 2, jnp.where(outer == 3, 0, jnp.where(outer == 1, 1, 3)))
    on_x, on_y = jnp.where(core == 0, outer, inner), jnp.where(core == 0, inner, outer)
    return ((y + on_y) % 4 * 4 + (x + on_x) % 4) * 16 + step % 16


def row_rows():
    z, core = lax.axis_index("z"), lax.axis_index("core")
    step = lax.broadcasted_iota(jnp.int32, (256, 1), 0)
    turn = step // 32 % 4
    to = jnp.where(turn % 2 == 0, z, 3 - z)
    to = jnp.where(turn < 2, to, to + 1 - to % 2 * 2)
    return (to * 2 + (core + step // 128) % 2) * 32 + step % 32


PARTS = tuple(range(0, 3200, 640))


def first_kernel(gate_proj, gate, up_proj, up, forth, back, gate_rest, up_rest, gate_kept, up_kept, projs, sems):
    proj_copies = [
        pltpu.make_async_copy(source, projs.at[index], sems.at[index]) for index, source in enumerate((gate_proj, up_proj))
    ]
    parts = ((0, 0, 1664), (0, 1664, 1536), (1, 0, 1664), (1, 1664, 1536))
    copies = []
    for number, (index, at, size) in enumerate(parts):
        source, target = ((gate, gate_kept), (up, up_kept))[index]
        to = pl.ds(at, size)
        copies.append(pltpu.make_async_copy(source.at[:, to], target.at[:, to], sems.at[2 + number]))
    for copy in proj_copies + copies:
        copy.start()
    rows = fsdp_rows()
    ordered = []
    for index, rest in enumerate((gate_rest, up_rest)):
        proj_copies[index].wait()
        ordered.append(picked(rows, projs[index], 1))
        rest[...] = ordered[index][64:]
    for copy, (index, start, size) in zip(copies, parts):
        copy.wait()
        kept = (gate_kept, up_kept)[index]
        for at in range(start, start + size, 512):
            width = min(512, start + size - at)
            part = jnp.dot(ordered[index][:64], kept[:, at : at + width], preferred_element_type=F32).astype(BF16)
            base = index * 3200 + at
            forth[:, base : base + width] = part[:32]
            back[:, base : base + width] = part[32:]


def rest_kernel(gate_rest, gate, up_rest, up, forth, back, near, far, keep):
    for rest, grad, base in ((gate_rest, gate, 0), (up_rest, up, 3200)):
        for at in range(0, 3200, 640):
            to = slice(base + at, base + at + 640)
            part = jnp.dot(rest[...], grad[:, at : at + 640], preferred_element_type=F32).astype(BF16)
            near[:, to] = part[:32]
            forth[:, to] = part[32:64]
            back[:, to] = part[64:96]
            far[:, to] = part[96:128]
            keep[:, to] = part[128:]


def pass_kernel(own, arrived, onward):
    onward[...] = wide(own[...], arrived[...]).astype(BF16)


def collect_kernel(keep, high_below, low_above, low, high):
    low[...] = wide(keep[:32], low_above[...])
    high[...] = wide(keep[32:], high_below[...])


def near_kernel(low, low_below, own, above):
    total = wide(low[...], low_below[...])
    own[...] = total[:16]
    above[...] = total[16:].astype(BF16)


def far_kernel(high, high_above, opposite, below):
    total = wide(high[...], high_above[...]).astype(BF16)
    opposite[...] = total[:16]
    below[...] = total[16:]


def moments(projected, first, second):
    return (
        beta_first * first[...] + (1.0 - beta_first) * projected,
        beta_second * second[...] + (1.0 - beta_second) * projected * projected,
    )


def channel_sums(projected, first, second):
    first_value, second_value = moments(projected, first, second)
    corrected = (first_value * (1.0 / (1.0 - beta_first**STEP))) / (
        jnp.sqrt(second_value * (1.0 / (1.0 - beta_second**STEP))) + adam_epsilon
    )
    return jnp.sum(corrected * corrected, 0, keepdims=True), jnp.sum(projected * projected, 0, keepdims=True)


def ready_kernel(own, arrived, first_gate, second_gate, first_up, second_up, total, first, second):
    total[...] = wide(own[...], arrived[...])
    for at, old_first, old_second in ((0, first_gate, second_gate), (3200, first_up, second_up)):
        first[:, at : at + 3200] = old_first[...] * (beta_first / (1.0 - beta_first**STEP))
        second[:, at : at + 3200] = old_second[...] * (beta_second / (1.0 - beta_second**STEP))


def pair_sum_kernel(own, a, b, first, second, sums, sent, total):
    projected = wide(own[...], a[...], b[...])
    total[...] = projected
    squared = projected * projected
    corrected = (first[...] + projected * ((1.0 - beta_first) / (1.0 - beta_first**STEP))) / (
        jnp.sqrt(second[...] + squared * ((1.0 - beta_second) / (1.0 - beta_second**STEP))) + adam_epsilon
    )
    corrected_sq = jnp.sum(corrected * corrected, 0, keepdims=True)
    projected_sq = jnp.sum(squared, 0, keepdims=True)
    sums[0:1], sums[1:2] = corrected_sq[:, :3200], projected_sq[:, :3200]
    sums[2:3], sums[3:4] = corrected_sq[:, 3200:], projected_sq[:, 3200:]
    sent[...] = sums[...].astype(BF16)


def moment_kernel(total, total_d, first_gate, second_gate, first_up, second_up, first_down, second_down, *news):
    news[0][...], news[1][...] = moments(total[:, :3200], first_gate, second_gate)
    news[2][...], news[3][...] = moments(total[:, 3200:], first_up, second_up)
    news[4][...], news[5][...] = moments(total_d[...], first_down, second_down)


def down_sum_kernel(own, other, first, second, sums, sent, total):
    projected = wide(own[...], other[:64])
    total[...] = projected[:32]
    near = channel_sums(projected[:32], first, second)
    far = channel_sums(projected[32:], other[64:96].astype(F32), other[96:].astype(F32))
    sums[...] = jnp.zeros_like(sums)
    sums[0:1], sums[1:2] = near[0] + far[0], near[1] + far[1]
    sent[...] = sums[...].astype(BF16)


def add_kernel(*refs):
    refs[-1][...] = wide(*(ref[...] for ref in refs[:-1]))


def sum_kernel(*refs):
    total = wide(*(ref[...] for ref in refs[:-2]))
    refs[-2][...] = total
    refs[-1][...] = total.astype(BF16)


def scale_of(corrected_sq, projected_sq):
    return update_scale * (jnp.sqrt(corrected_sq) / (jnp.sqrt(projected_sq) + norm_epsilon))


def update_kernel(gate, up, own, other, gate_out, up_out, gate_made, up_made, sems):
    sums = wide(own[...], other[...])
    copies = []
    for index, (grad, made, out) in enumerate(((gate, gate_made, gate_out), (up, up_made, up_out))):
        scale = scale_of(sums[2 * index : 2 * index + 1], sums[2 * index + 1 : 2 * index + 2])
        made[...] = (grad[...].astype(F32) * scale).astype(BF16)
        copies.append(pltpu.make_async_copy(made, out, sems.at[index]))
        copies[-1].start()
    for copy in copies:
        copy.wait()


def down_kernel(proj, grad, own, other):
    ordered = picked(row_rows(), proj[...], 0)
    for at, size in ((0, 512), (512, 512), (1024, 576)):
        part = lax.dot_general(
            ordered, grad[at : at + size], (((1,), (1,)), ((), ())), preferred_element_type=F32
        ).astype(BF16)
        own[:, at : at + size] = part[:128]
        other[:, at : at + size] = part[128:]


def down_split_kernel(own, other, keep, send):
    total = wide(own[...], other[...])
    keep[...] = total[:64]
    send[...] = total[64:].astype(BF16)


def down_halve_kernel(own, other, first, second, keep, send):
    total = wide(own[...], other[...])
    keep[...] = total
    send[:32] = total[32:].astype(BF16)
    send[32:64] = total[:32].astype(BF16)
    send[64:96] = first[...].astype(BF16)
    send[96:] = second[...].astype(BF16)


def down_update_kernel(grad, own, other, out, scale):
    sums = wide(own[...], other[...])
    scale[:, :1600] = scale_of(sums[0:1], sums[1:2])
    for at in range(0, 1600, 128):
        size = min(128, 1600 - at)
        column = jnp.broadcast_to(scale[:, at : at + 128], (128, 128)).T[:size]
        for lane in range(0, 640, 128):
            block = grad[at : at + size, lane : lane + 128].astype(F32) * column
            out[at : at + size, lane : lane + 128] = block.astype(BF16)


def per_device(
    grad_gate,
    grad_up,
    grad_down,
    proj_gate,
    proj_up,
    proj_down,
    first_gate,
    second_gate,
    first_up,
    second_up,
    first_down,
    second_down,
):
    gate, up, down = grad_gate.T, grad_up.T, grad_down.T
    run = Chain()
    half, piece = pltpu.VMEM((32, 6400), BF16), pltpu.VMEM((16, 6400), BF16)
    part, held = pltpu.VMEM((192, 320), BF16), pltpu.VMEM((320, 3200), BF16)
    row, pair_row = pltpu.VMEM((8, 1600), F32), pltpu.VMEM((4, 3200), F32)
    sent_row, sent_pair = pltpu.VMEM((8, 1600), BF16), pltpu.VMEM((4, 3200), BF16)
    whole = jax.ShapeDtypeStruct((320, 3200), BF16)
    state, down_state = jax.ShapeDtypeStruct((16, 3200), F32), jax.ShapeDtypeStruct((32, 1600), F32)

    forth, back, rest_g, rest_u, gate, up = run(
        first_kernel,
        (half, half, part, part, held, held),
        proj_gate.T, gate, proj_up.T, up,
        in_specs=(HBM,) * 4,
        scratch=(pltpu.VMEM((2, 320, 256), BF16), pltpu.SemaphoreType.DMA((6,))),
    )
    from_below, from_above = ring_send(forth, 1, 0), ring_send(back, 3, 0)
    forth, back, near, far, keep = run(
        rest_kernel, (half, half, half, half, pltpu.VMEM((64, 6400), BF16)), rest_g, gate, rest_u, up
    )
    high_below, low_above = ring_send(forth, 1, 0), ring_send(back, 3, 0)
    own_down, other_down = run(down_kernel, (pltpu.VMEM((128, 1600), BF16),) * 2, proj_down, down)
    other_down = core_send(other_down)
    (forth,) = run(pass_kernel, (half,), near, from_below)
    low_below = ring_send(forth, 1, 0)
    (back,) = run(pass_kernel, (half,), far, from_above)
    high_above = ring_send(back, 3, 0)
    low, high = run(collect_kernel, (pltpu.VMEM((32, 6400), F32),) * 2, keep, high_below, low_above)
    own_down, other_down = run(
        down_split_kernel, (pltpu.VMEM((64, 1600), F32), pltpu.VMEM((64, 1600), BF16)), own_down, other_down
    )
    other_down = z_swap(other_down, False)

    own, above = run(near_kernel, (pltpu.VMEM((16, 6400), F32), piece), low, low_below)
    above = ring_send(above, 1, 1)
    opposite, below = run(far_kernel, (piece, piece), high, high_above)
    opposite, below = ring_send(opposite, 2, 1), ring_send(below, 3, 1)
    own_down, other_down = run(
        down_halve_kernel,
        (pltpu.VMEM((64, 1600), F32), pltpu.VMEM((128, 1600), BF16)),
        own_down, other_down, first_down, second_down,
    )
    other_down = z_swap(other_down, True)

    states = (first_gate, second_gate, first_up, second_up)
    own, old_first, old_second = run(ready_kernel, (pltpu.VMEM((16, 6400), F32),) * 3, own, above, *states)
    sums, sent, total = run(
        pair_sum_kernel, (pair_row, sent_pair, pltpu.VMEM((16, 6400), F32)), own, below, opposite, old_first, old_second,
        cost=8 * 10**9,
    )
    other = ring_swap(sent, False, 1)
    sums, sent = run(sum_kernel, (pair_row, sent_pair), sums, other)
    other = ring_swap(sent, True, 1)
    sums_d, sent_d, total_d = run(
        down_sum_kernel, (row, sent_row, pltpu.VMEM((32, 1600), F32)), own_down, other_down, first_down, second_down
    )
    other_d = z_swap(sent_d, False)
    sums, sent = run(sum_kernel, (pair_row, sent_pair), sums, other)
    other = ring_swap(sent, False, 0)
    sums_d, sent_d = run(sum_kernel, (row, sent_row), sums_d, other_d)
    other_d = core_send(sent_d)
    news = run(moment_kernel, (state,) * 4 + (down_state,) * 2, total, total_d, *states, first_down, second_down)
    sums, sent = run(sum_kernel, (pair_row, sent_pair), sums, other)
    other = ring_swap(sent, True, 0)
    (update_down,) = run(
        down_update_kernel,
        (jax.ShapeDtypeStruct((1600, 640), BF16),),
        down, sums_d, other_d,
        scratch=(pltpu.VMEM((1, 1664), F32),),
    )
    update_gate, update_up = run(
        update_kernel,
        (whole, whole),
        gate, up, sums, other,
        out_specs=(HBM, HBM),
        scratch=(held, held, pltpu.SemaphoreType.DMA((2,))),
        last=True,
    )
    return (
        update_gate.T,
        update_up.T,
        update_down.T,
        *news,
    )


def solution(mesh):
    fine = Mesh(mesh.devices.reshape(SIZES), AXES)
    gradient, state = P(ACROSS, ALONG), P(ALONG, ACROSS)
    return jax.shard_map(
        per_device,
        mesh=fine,
        in_specs=(
            gradient,
            gradient,
            gradient,
            P(None, ALONG),
            P(None, ALONG),
            P(None, ACROSS),
            state,
            state,
            state,
            state,
            gradient,
            gradient,
        ),
        out_specs=(
            gradient,
            gradient,
            gradient,
            state,
            state,
            state,
            state,
            gradient,
            gradient,
        ),
        check_vma=False,
    )
```
